128 devices in a mesh: aln: 2 (over core), col: 64 (over y, z, x).
Axes of the slice: x: 4, y: 4, z: 4, core: 2. Of those that a mesh axis runs over, the one named last changes fastest.
Arguments:
- inputs: bfloat16 [2, 64, 512, 768], P('aln', None, 'col'), may hold values from -6 to 6
- gap_flags: int32 [2, 64, 512], P('aln', None, 'col'), may hold values 0 or 1
- band_mask: int32 [2, 512, 65], P('aln', 'col'), may hold values 0 or 1
- row_gain: float32 [768], replicated, may hold values from 0.5 to 1.5
- row_shift: float32 [768], replicated, may hold values from -2 to 2
- row_query: bfloat16 [768, 768], replicated, may hold values from -0.21875 to 0.21875
- row_key: bfloat16 [768, 768], replicated, may hold values from -0.21875 to 0.21875
- row_value: bfloat16 [768, 768], replicated, may hold values from -0.21875 to 0.21875
- row_out: bfloat16 [768, 768], replicated, may hold values from -1.25 to 1.25
- col_gain: float32 [768], replicated, may hold values from 0.5 to 1.5
- col_shift: float32 [768], replicated, may hold values from -2 to 2
- col_query: bfloat16 [768, 768], replicated, may hold values from -0.21875 to 0.21875
- col_key: bfloat16 [768, 768], replicated, may hold values from -0.21875 to 0.21875
- col_value: bfloat16 [768, 768], replicated, may hold values from -0.21875 to 0.21875
- col_out: bfloat16 [768, 768], replicated, may hold values from -1.25 to 1.25
- mlp_gain: float32 [768], replicated, may hold values from 0.5 to 1.5
- mlp_shift: float32 [768], replicated, may hold values from -2 to 2
- mlp_up: bfloat16 [768, 3072], replicated, may hold values from -0.21875 to 0.21875
- up_bias: float32 [3072], replicated, may hold values from -3 to 3
- mlp_down: bfloat16 [3072, 768], replicated, may hold values from -0.109375 to 0.109375
- down_bias: float32 [768], replicated, may hold values from -2 to 2
- cotangent: bfloat16 [2, 64, 512, 768], P('aln', None, 'col'), may hold values from -6 to 6
Outputs:
- result: bfloat16 [2, 64, 512, 768], P('aln', None, 'col')
- grad_inputs: float32 [2, 64, 512, 768], P('aln', None, 'col')
- grad_row_gain: float32 [768], P('aln')
- grad_row_shift: float32 [768], P('aln')
- grad_row_query: float32 [768, 768], P('aln')
- grad_row_key: float32 [768, 768], P('aln')
- grad_row_value: float32 [768, 768], P('aln')
- grad_row_out: float32 [768, 768], P('aln')
- grad_col_gain: float32 [768], P('aln')
- grad_col_shift: float32 [768], P('aln')
- grad_col_query: float32 [768, 768], P('aln')
- grad_col_key: float32 [768, 768], P('aln')
- grad_col_value: float32 [768, 768], P('aln')
- grad_col_out: float32 [768, 768], P('aln')
- grad_mlp_gain: float32 [768], P('aln')
- grad_mlp_shift: float32 [768], P('aln')
- grad_mlp_up: float32 [768, 3072], P('aln')
- grad_up_bias: float32 [3072], P('aln')
- grad_mlp_down: float32 [3072, 768], P('aln')
- grad_down_bias: float32 [768], P('aln')
The draws below stay inside these ranges and needn't reach their ends.
All inputs are finite; a program needn't handle non-finite values. No bound on the sum of `gap_flags` or of `band_mask` on one device may be relied on, other than what follows from the above.
Results may differ from the reference program's by a relative error of at most 0.025.
Values may be sent and summed in bfloat16 or wider, within the bound.
A program may use at most 320 MiB of HBM per device.

```python
import math
import jax
import jax.numpy as jnp
from jax import lax

D = 768
H = 12
HD = 64
FF = 3072
S = 64
COLS = 512
BAND = 32
ALIGN = 2


def with_ends(result, key, low, top_value):
    extent = result.shape
    place = [jax.random.randint(jax.random.fold_in(key, axis), (), 0, extent[axis]) for axis in range(len(extent))]
    result = result.at[tuple(place)].set(low)
    longest = extent.index(max(extent))
    place[longest] = (place[longest] + 1) % extent[longest]
    return result.at[tuple(place)].set(top_value)


def shard_levels(rng, extent, split, smallest, high):
    factor_of = 1.0
    for axis_at, blocks in split:
        heights = jax.random.uniform(jax.random.fold_in(jax.random.fold_in(rng, 6), axis_at), (blocks,), jnp.float32, smallest / len(split), high / len(split))
        factor_of = factor_of * jnp.repeat(jnp.exp(heights), extent[axis_at] // blocks).reshape((-1,) + (1,) * (len(extent) - 1 - axis_at))
    return factor_of


def bell_draw(stream_key, dims, scale, limit, pieces=(), held_as=jnp.bfloat16):
    entries = scale * jax.random.normal(stream_key, dims, jnp.float32)
    if pieces:
        entries = entries * shard_levels(stream_key, dims, pieces, -0.22, 0.18)
    return jnp.clip(entries, -limit, limit).astype(held_as)


def setup_inputs(seed: int = 0) -> dict:
    keys = jax.random.split(jax.random.key(seed), 23)
    return {
        "inputs": bell_draw(keys[0], (ALIGN, S, COLS, D), 1.0, 6.0, ((0, 2), (2, 64))),
        "gap_flags": with_ends((jax.random.randint(keys[1], (ALIGN, S, COLS), 0, 4) < 1).astype(jnp.int32), jax.random.fold_in(keys[1], 1), 0, 1),
        "band_mask": with_ends((jax.random.randint(keys[2], (ALIGN, COLS, 2 * BAND + 1), 0, 2) < 1).astype(jnp.int32), jax.random.fold_in(keys[2], 1), 0, 1),
        "row_gain": jnp.clip(1.0 + 0.1 * jax.random.normal(keys[3], (D,), jnp.float32), 0.5, 1.5),
        "row_shift": bell_draw(keys[4], (D,), 0.3, 2.0, (), jnp.float32),
        "row_query": bell_draw(keys[5], (D, D), D ** -0.5, 0.21875),
        "row_key": bell_draw(keys[6], (D, D), D ** -0.5, 0.21875),
        "row_value": bell_draw(keys[7], (D, D), D ** -0.5, 0.21875),
        "row_out": bell_draw(keys[8], (D, D), (D // 32) ** -0.5, 1.25),
        "col_gain": jnp.clip(1.0 + 0.1 * jax.random.normal(keys[9], (D,), jnp.float32), 0.5, 1.5),
        "col_shift": bell_draw(keys[10], (D,), 0.3, 2.0, (), jnp.float32),
        "col_query": bell_draw(keys[11], (D, D), D ** -0.5, 0.21875),
        "col_key": bell_draw(keys[12], (D, D), D ** -0.5, 0.21875),
        "col_value": bell_draw(keys[13], (D, D), D ** -0.5, 0.21875),
        "col_out": bell_draw(keys[14], (D, D), (D // 32) ** -0.5, 1.25),
        "mlp_gain": jnp.clip(1.0 + 0.1 * jax.random.normal(keys[15], (D,), jnp.float32), 0.5, 1.5),
        "mlp_shift": bell_draw(keys[16], (D,), 0.3, 2.0, (), jnp.float32),
        "mlp_up": bell_draw(keys[17], (D, FF), D ** -0.5, 0.21875),
        "up_bias": bell_draw(keys[18], (FF,), 0.5, 3.0, (), jnp.float32),
        "mlp_down": bell_draw(keys[19], (FF, D), FF ** -0.5, 0.109375),
        "down_bias": bell_draw(keys[20], (D,), 0.3, 2.0, (), jnp.float32),
        "cotangent": bell_draw(keys[21], (ALIGN, S, COLS, D), 1.0, 6.0, ((0, 2), (2, 64))),
    }


GAP_DROP = 0.75
EPSILON = 1e-05
NEG_FILL = -1000000000.0

@jax.custom_vjp
def low(v):
    return lax.optimization_barrier(v.astype(jnp.bfloat16)).astype(jnp.float32)

@jax.custom_vjp
def low_back(v):
    return v

def low_keep(v):
    return (low(v), None)

def low_pass(kept, grad):
    return (grad,)

def back_keep(v):
    return (v, None)

def back_low(kept, grad):
    return (low(grad),)
low.defvjp(low_keep, low_pass)
low_back.defvjp(back_keep, back_low)

def mixes(left, right):
    return jnp.einsum('scd,de->sce', left, right, precision=lax.Precision.HIGHEST)

def normalize(values, gain, shift):
    center = values - lax.optimization_barrier(jnp.mean(values, axis=-1, keepdims=True))
    spread = lax.optimization_barrier(jnp.mean(center * center, axis=-1, keepdims=True))
    return center * lax.rsqrt(spread + EPSILON) * gain + shift

def layer_one(values, flags, bands, params):
    row_gain, row_shift, row_query, row_key, row_value, row_out, col_gain, col_shift, col_query, col_key, col_value, col_out, mlp_gain, mlp_shift, mlp_up, up_bias, mlp_down, down_bias = params
    highest = lax.Precision.HIGHEST
    weight_gap = (1.0 - GAP_DROP * flags.astype(jnp.float32))[:, :, None]
    normed = low(normalize(values, row_gain, row_shift))
    queries = low(weight_gap * low_back(mixes(normed, row_query))).reshape(S, COLS, H, HD)
    keyset = low(weight_gap * low_back(mixes(normed, row_key))).reshape(S, COLS, H, HD)
    valueset = low(low_back(mixes(normed, row_value))).reshape(S, COLS, H, HD)
    scores = jnp.einsum('sihe,sjhe->hij', queries, keyset, precision=highest) * (1.0 / math.sqrt(HD * S))
    scores = low_back(scores)
    offsets = (jnp.arange(COLS)[None, :] - jnp.arange(COLS)[:, None] + BAND).astype(jnp.int32)
    inside = (offsets >= 0) & (offsets <= 2 * BAND)
    picked = jnp.take_along_axis(bands, jnp.clip(offsets, 0, 2 * BAND), axis=1)
    allowed = inside & ((picked == 1) | (offsets == BAND))
    probs = jax.nn.softmax(jnp.where(allowed[None], scores, NEG_FILL), axis=-1)
    mixed = jnp.einsum('hij,sjhe->sihe', low(probs), valueset, precision=highest)
    mixed = low(low_back(mixed)).reshape(S, COLS, D)
    after_row = values + low_back(mixes(mixed, row_out))
    normed_col = low(normalize(after_row, col_gain, col_shift))
    cross_queries = low(low_back(mixes(normed_col, col_query))).reshape(S, COLS, H, HD)
    cross_keys = low(low_back(mixes(normed_col, col_key))).reshape(S, COLS, H, HD)
    cross_values = low(low_back(mixes(normed_col, col_value))).reshape(S, COLS, H, HD)
    col_scores = jnp.einsum('sche,tche->chst', cross_queries, cross_keys, precision=highest) * (1.0 / math.sqrt(HD))
    col_probs = jax.nn.softmax(low_back(col_scores), axis=-1)
    col_mixed = jnp.einsum('chst,tche->sche', low(col_probs), cross_values, precision=highest)
    col_mixed = low(low_back(col_mixed)).reshape(S, COLS, D)
    after_col = after_row + low_back(mixes(col_mixed, col_out))
    normed_mlp = low(normalize(after_col, mlp_gain, mlp_shift))
    hidden = low(jax.nn.gelu(low_back(mixes(normed_mlp, mlp_up) + up_bias), approximate=False))
    return after_col + low_back(mixes(hidden, mlp_down) + down_bias)

def reference(inputs, gap_flags, band_mask, row_gain, row_shift, row_query, row_key, row_value, row_out, col_gain, col_shift, col_query, col_key, col_value, col_out, mlp_gain, mlp_shift, mlp_up, up_bias, mlp_down, down_bias, cotangent):
    floats = tuple((weight.astype(jnp.float32) for weight in (row_gain, row_shift, row_query, row_key, row_value, row_out, col_gain, col_shift, col_query, col_key, col_value, col_out, mlp_gain, mlp_shift, mlp_up, up_bias, mlp_down, down_bias)))

    def forward(values, *params):
        stepper = jax.checkpoint(lambda bundle: layer_one(bundle[0], bundle[1], bundle[2], params))
        return lax.map(stepper, (values, gap_flags, band_mask))
    output, pullback = jax.vjp(forward, inputs.astype(jnp.float32), *floats)
    grads = pullback(cotangent.astype(jnp.float32))
    return (output.astype(jnp.bfloat16), grads[0], grads[1], grads[2], grads[3], grads[4], grads[5], grads[6], grads[7], grads[8], grads[9], grads[10], grads[11], grads[12], grads[13], grads[14], grads[15], grads[16], grads[17], grads[18])
```

```python
import functools
import math

import jax
import jax.numpy as jnp
from jax import lax
from jax.experimental import pallas as pl
from jax.experimental.pallas import tpu as pltpu
from jax.sharding import PartitionSpec as P

H = 12
HD = 64
COLS = 512
BAND = 32


GAP_DROP = 0.75
MESH = pl.DeviceIdType.MESH
LANES = 768
HALF = 384
QUARTER = 96
PIECE = 48
BF = jnp.bfloat16
F32 = jnp.float32


def place():
    col = lax.axis_index("col")
    return {
        "aln": lax.axis_index("aln"),
        "x": lax.rem(col, 4),
        "z": lax.rem(lax.div(col, 4), 4),
        "y": lax.div(col, 16),
    }


def device_at(spot):
    return (spot["aln"], spot["y"] * 16 + spot["z"] * 4 + spot["x"])


def mod4(v):
    return lax.rem(v + 4, 4)


def shifted(spot, axis, step):
    if axis == "aln":
        return device_at({**spot, "aln": 1 - spot["aln"]})
    return device_at({**spot, axis: mod4(spot[axis] + step)})


def greet(spot, reach):
    barrier = pltpu.get_barrier_semaphore()
    for peer in reach:
        pl.semaphore_signal(barrier, inc=1, device_id=peer, device_id_type=MESH)
    pl.semaphore_wait(barrier, len(reach))


def torus_reach(spot):
    return [shifted(spot, a, s) for a in "xyz" for s in (1, 2, 3)] + [shifted(spot, "aln", 1)]


def block(rows, count, lanes=0, width=LANES):
    return (pl.ds(pl.multiple_of(rows, 16), count), pl.ds(pl.multiple_of(lanes, 128), width))


def add_into(dst, at, sources):
    total = dst[at]
    for ref, near in sources:
        total = total + ref[near]
    dst[at] = total


class Copies:
    def __init__(self, send_sem, recv_sem):
        self.send_sem, self.recv_sem, self.used, self.sent = send_sem, recv_sem, 0, []

    def start(self, src, dst, device):
        k = self.used
        self.used += 1
        copy = pltpu.make_async_remote_copy(
            src_ref=src, dst_ref=dst, send_sem=self.send_sem.at[k], recv_sem=self.recv_sem.at[k],
            device_id=device, device_id_type=MESH)
        copy.start()
        self.sent.append(copy)
        return copy

    def finish(self):
        for copy in self.sent:
            copy.wait_send()
        self.sent = []


def wait_all(started):
    for copy in started:
        copy.wait_recv()


UNIT_COPIES = 20


def reduce_unit(spot, copies, load, give, total, base, swap, recv, pieces, out, store_sem, order):
    first, second, third = order
    got = copies.start(give, swap, shifted(spot, "aln", 1))
    yield
    load()
    got.wait_recv()
    for r in range(4):
        add_into(total, block(base + QUARTER * r, QUARTER), [(swap, block(QUARTER * r, QUARTER))])
    m = spot[first]
    up, down = shifted(spot, first, 1), shifted(spot, first, -1)

    def chunk(k, lane):
        return block(base + mod4(k) * QUARTER, QUARTER, lane, HALF)

    def slot(j):
        return block(QUARTER * (j % 3), QUARTER, HALF * (j // 3), HALF)

    relay_up = copies.start(total.at[chunk(m + 2, 0)], recv.at[slot(0)], up)
    relay_down = copies.start(total.at[chunk(m + 2, HALF)], recv.at[slot(3)], down)
    early_up = copies.start(total.at[chunk(m + 1, HALF)], recv.at[slot(1)], up)
    early_down = copies.start(total.at[chunk(m - 1, 0)], recv.at[slot(4)], down)
    yield
    relay_up.wait_recv()
    add_into(total, chunk(m + 1, 0), [(recv, slot(0))])
    late_up = copies.start(total.at[chunk(m + 1, 0)], recv.at[slot(2)], up)
    relay_down.wait_recv()
    add_into(total, chunk(m - 1, HALF), [(recv, slot(3))])
    late_down = copies.start(total.at[chunk(m - 1, HALF)], recv.at[slot(5)], down)
    yield
    wait_all([early_up, early_down, late_up, late_down])
    add_into(total, chunk(m, 0), [(recv, slot(2)), (recv, slot(4))])
    add_into(total, chunk(m, HALF), [(recv, slot(1)), (recv, slot(5))])
    mine = base + m * QUARTER
    n = spot[second]

    def piece(k, start=mine):
        return block(start + lax.div(mod4(k), 2) * PIECE, PIECE, lax.rem(mod4(k), 2) * HALF, HALF)

    got = [copies.start(total.at[piece(n + d)], pieces.at[d - 1], shifted(spot, second, d)) for d in (1, 2, 3)]
    yield
    wait_all(got)
    own = total[piece(n)].astype(F32)
    for d in range(3):
        own = own + pieces[d].astype(F32)
    spread = spot[third]
    pieces[3 + spread] = own.astype(BF)
    got = [copies.start(pieces.at[3 + spread], pieces.at[3 + spread], shifted(spot, third, d)) for d in (1, 2, 3)]
    yield
    wait_all(got)
    own = pieces[3].astype(F32)
    for d in range(1, 4):
        own = own + pieces[3 + d].astype(F32)
    total[piece(n)] = own.astype(BF)
    here = m * QUARTER
    store = pltpu.make_async_copy(total.at[piece(n)], out.at[piece(n, here)], store_sem)
    store.start()
    got = [copies.start(total.at[piece(n)], out.at[piece(n, here)], shifted(spot, second, d)) for d in (1, 2, 3)]
    yield
    store.wait()
    wait_all(got)

    def whole(k, lane=0, width=LANES):
        return out.at[block(mod4(k) * QUARTER, QUARTER, lane, width)]

    go_up = copies.start(whole(m), whole(m), up)
    go_down = copies.start(whole(m), whole(m), down)
    yield
    go_up.wait_recv()
    on_up = copies.start(whole(m - 1, 0, HALF), whole(m - 1, 0, HALF), up)
    go_down.wait_recv()
    on_down = copies.start(whole(m + 1, HALF, HALF), whole(m + 1, HALF, HALF), down)
    yield
    wait_all([on_up, on_down])


def sum_small(spot, copies, small, halves, slots):
    mine, other = spot["aln"], 1 - spot["aln"]

    def half(which):
        return (slice(None), pl.ds(pl.multiple_of(which * HALF, HALF), HALF))

    swap = copies.start(small.at[half(other)], slots.at[12], shifted(spot, "aln", 1))
    yield
    swap.wait_recv()
    halves[0] = small[half(mine)] + slots[12]
    for n, axis in enumerate(("x", "y", "z")):
        m = spot[axis]
        slots[4 * n + m] = halves[n]
        got = [copies.start(slots.at[4 * n + m], slots.at[4 * n + m], shifted(spot, axis, k)) for k in (1, 2, 3)]
        yield
        wait_all(got)
        halves[n + 1] = (slots[4 * n] + slots[4 * n + 1]) + (slots[4 * n + 2] + slots[4 * n + 3])


SMALL_COPIES = 10


class Run:
    def __init__(self, steps):
        self.steps, self.live = steps, True

    def step(self):
        if self.live:
            self.live = next(self.steps, "end") != "end"


def step_all(*runs):
    for run in runs:
        run.step()


def finish_all(*runs):
    while any(run.live for run in runs):
        step_all(*runs)


def vector_rows(scratch, vectors):
    for n, vector in enumerate(vectors):
        scratch[n : n + 1, :] = vector[...].reshape(1, LANES)


class Stores:
    def __init__(self, sems):
        self.sems, self.copies = sems, []

    def start(self, src, dst):
        copy = pltpu.make_async_copy(src, dst, self.sems.at[len(self.copies)])
        copy.start()
        self.copies.append(copy)
        return copy

    def finish(self):
        for copy in self.copies:
            copy.wait()


def unit_scratch(count, own):
    return [
        pltpu.VMEM((max(own, 1), HALF, LANES), BF),
        pltpu.VMEM((count, HALF, LANES), BF),
        pltpu.VMEM((count, 3 * QUARTER, LANES), BF),
        pltpu.VMEM((count, 7, PIECE, HALF), BF),
        pltpu.SemaphoreType.DMA((count,)),
        pltpu.SemaphoreType.DMA((count,)),
    ]


def start_unit(spot, copies, scratch, n, give, keep, out, order):
    total, swap, recv, pieces, load_sem, store_sem = scratch
    copy = pltpu.make_async_copy(keep, total.at[n], load_sem.at[n])
    copy.start()
    return Run(reduce_unit(
        spot, copies, copy.wait, give, total.at[n], 0, swap.at[n], recv.at[n], pieces.at[n], out, store_sem.at[n], order))


GROUP = 16
SLAB = 128
REACH = 192
EPSILON = 1e-05
NEG_FILL = -1000000000.0


def dot_nn(a, b):
    return lax.dot_general(a, b, (((1,), (0,)), ((), ())), preferred_element_type=F32)


def dot_nt(a, b):
    return lax.dot_general(a, b, (((1,), (1,)), ((), ())), preferred_element_type=F32)


def dot_tn(a, b):
    return lax.dot_general(a, b, (((0,), (0,)), ((), ())), preferred_element_type=F32)


def quad_masks(dtype):
    lane = lax.broadcasted_iota(jnp.int32, (1, 256), 1)
    return [((lane >= 64 * h) & (lane < 64 * h + 64)).astype(F32).astype(dtype) for h in range(4)]


def spread_heads(block, masks):
    return jnp.concatenate([block * m for m in masks], axis=0)


def gather_heads(block, masks):
    n = block.shape[0] // 4
    out = block[0:n] * masks[0]
    for h in range(1, 4):
        out = out + block[n * h : n * h + n] * masks[h]
    return out


SLAB_ORDER = (1, 4, 3, 12, 2, 8, 5, 7, 13, 15, 6, 9, 11, 14, 10)


def slab_place(spot):
    return spot["z"] * 4 + spot["x"]


def slab_peer(spot, k):
    dz, dx = k // 4, k % 4
    there = {**spot, "z": mod4(spot["z"] + dz), "x": mod4(spot["x"] + dx)}
    return device_at(there), slab_place(there)


def exchange(spot, copies, src_of, dst_of):
    out = []
    for k in SLAB_ORDER:
        device, index = slab_peer(spot, k)
        out.append(copies.start(src_of(index), dst_of(slab_place(spot), k), device))
    return out


def slab_reach(spot):
    return [slab_peer(spot, k)[0] for k in range(1, GROUP)] + [shifted(spot, "y", 1), shifted(spot, "y", -1)]


def centre(rows):
    center = rows - jnp.mean(rows, axis=-1, keepdims=True)
    inverse = lax.rsqrt(jnp.mean(center * center, axis=-1, keepdims=True) + EPSILON)
    return center * inverse, inverse


def wide(weights):
    return jnp.concatenate([weights, weights], axis=1)


def row_forward_kernel(
    scale, x, aux, wq, wk, wv, row_gain, row_shift,
    mixed, xrow_out, q_out, kx_out, vx_out, probs_out, own, gaps_out,
    xin, auxin, weights, act, masks_in, mask_pick, scores, arrived, outgoing, xrow, q, kx, vx, probs, gaps, vecs,
    send_sem, recv_sem, local_sem, store_sem,
):
    spot = place()
    g = slab_place(spot)
    copies = Copies(send_sem, recv_sem)
    stores = Stores(store_sem)
    locals_ = [
        pltpu.make_async_copy(aux.at[g], auxin.at[g], local_sem.at[0]),
        pltpu.make_async_copy(x.at[g], xin.at[g], local_sem.at[1]),
        pltpu.make_async_copy(wk, weights.at[0], local_sem.at[2]),
        pltpu.make_async_copy(wv, weights.at[1], local_sem.at[3]),
        pltpu.make_async_copy(wq, weights.at[2], local_sem.at[4]),
    ]
    for copy in locals_:
        copy.start()
    vector_rows(vecs, (row_gain, row_shift))
    gain, shift = vecs.at[0:1], vecs.at[1:2]
    greet(spot, slab_reach(spot))
    got_aux = exchange(spot, copies, lambda i: aux.at[i], lambda me, k: auxin.at[me])
    got = exchange(spot, copies, lambda i: x.at[i], lambda me, k: xin.at[me])
    locals_[0].wait()
    locals_[1].wait()
    wait_all(got_aux)

    def regroup_row(row):
        def body(h, carry):
            k = 2 * row + h
            first = xin[2 * k].astype(F32)
            second = xin[2 * k + 1].astype(F32)
            side = auxin[2 * k].astype(F32)
            other = auxin[2 * k + 1].astype(F32)
            for s in range(4):
                rows = jnp.concatenate([first[8 * s : 8 * s + 8], second[8 * s : 8 * s + 8]], axis=0)
                at = pl.ds(pl.multiple_of(SLAB * s + 16 * k, 16), 16)
                xrow[at, :] = rows.astype(BF)
                scaled, _ = centre(rows)
                act[at, :] = (scaled * gain[...] + shift[...]).astype(BF)
                gaps[at, :] = jnp.concatenate([side[8 * s : 8 * s + 8], other[8 * s : 8 * s + 8]], axis=0)
            at = pl.ds(pl.multiple_of(16 * k, 16), 16)
            masks_in[at, :] = jnp.concatenate([side[32:40], other[32:40]], axis=0)
            return carry

        lax.fori_loop(0, 2, body, 0)

    by_step = dict(zip(SLAB_ORDER, got))
    for dz in (0, 3, 1, 2):
        wait_all([by_step[4 * dz + dx] for dx in range(4) if 4 * dz + dx > 0])
        regroup_row(mod4(spot["z"] - dz))
    stores.start(xrow, xrow_out)
    stores.start(gaps, gaps_out)
    halos = []
    up, down = shifted(spot, "y", 1), shifted(spot, "y", -1)

    def project(which):
        target = (kx, vx)[which]
        locals_[2 + which].wait()
        for lanes in THIRDS:
            made = dot_nn(act[...], weights[which, :, lanes])
            if which == 0:
                made = made * wide(gaps[...])
            for s in range(4):
                target[s, 32:160, lanes] = made[SLAB * s : SLAB * s + SLAB].astype(BF)
        halos.append([
            copies.start(target.at[:, 128:160], target.at[:, 0:32], up),
            copies.start(target.at[:, 32:64], target.at[:, 160:192], down),
        ])

    project(0)
    locals_[4].wait()
    for lanes in THIRDS:
        q[:, lanes] = (dot_nn(act[...], weights[2, :, lanes]) * wide(gaps[...])).astype(BF)
    stores.start(q, q_out)
    wait_all(halos[0])
    stores.start(kx, kx_out)
    picks = quad_masks(BF)
    for b in range(2):
        for n in range(3):
            lanes = THIRDS[n]
            total = None
            for s in range(4):
                heads = spread_heads(q[SLAB * s + 64 * b : SLAB * s + 64 * b + 64, lanes], picks)
                term = dot_nt(heads, kx[s, 64 * b : 64 * b + 128, lanes])
                total = term if total is None else total + term
            scores[256 * (3 * b + n) : 256 * (3 * b + n) + 256, :] = total
    got = exchange(spot, copies, lambda i: scores.at[pl.ds(pl.multiple_of(96 * i, 32), 96)], lambda me, k: arrived.at[k])
    project(1)
    rows = masks_in[pl.ds(pl.multiple_of(64 * lax.div(g, 8), 64), 64), :]
    mask_pick[0:64, :] = rows
    mask_pick[64:128, :] = rows
    allowed = mask_pick[pl.ds(pl.multiple_of(32 * lax.rem(g, 2), 32), 96), :]
    wait_all(got)
    mine = pl.ds(pl.multiple_of(96 * g, 32), 96)
    total = scores[mine, :]
    for k in range(1, GROUP):
        total = total + arrived[k]
    total = jnp.where(allowed > 0.5, total * scale, NEG_FILL)
    expo = jnp.exp(total - jnp.max(total, axis=-1, keepdims=True))
    share = expo / jnp.sum(expo, axis=-1, keepdims=True)
    probs[mine, :] = share.astype(BF)
    got = exchange(spot, copies, lambda i: probs.at[mine], lambda me, k: probs.at[mine])
    own[...] = share
    wait_all(halos[1])
    stores.start(vx, vx_out)
    wait_all(got)
    stores.start(probs, probs_out)
    picks = quad_masks(F32)
    at = pl.ds(pl.multiple_of(32 * g, 32), 32)
    got = []
    for dz in (1, 3, 2, 0):
        target = mod4(spot["z"] + dz)
        b, low = lax.div(target, 2), 32 * lax.rem(target, 2)
        for n, lanes in enumerate(THIRDS):
            weigh = jnp.concatenate(
                [probs[pl.ds(pl.multiple_of(256 * (3 * b + n) + 64 * h + low, 32), 32), :] for h in range(4)], axis=0
            )
            for pair in range(2):
                made = [
                    gather_heads(
                        dot_nn(weigh, vx[2 * pair + t, pl.ds(pl.multiple_of(64 * b, 64), 128), lanes]), picks
                    )
                    for t in range(2)
                ]
                for j in range(4):
                    outgoing[4 * target + j, 16 * pair : 16 * pair + 16, lanes] = jnp.concatenate(
                        [m[8 * j : 8 * j + 8] for m in made], axis=0
                    ).astype(BF)
        for dx in range(4):
            if 4 * dz + dx > 0:
                device, index = slab_peer(spot, 4 * dz + dx)
                got.append(copies.start(outgoing.at[index], mixed.at[at], device))
    stores.start(outgoing.at[g], mixed.at[at])
    wait_all(got)
    copies.finish()
    stores.finish()


def vmem_spec():
    return pl.BlockSpec(memory_space=pltpu.VMEM)


def any_spec():
    return pl.BlockSpec(memory_space=pl.ANY)


def row_forward(x, aux, wq, wk, wv, row_gain, row_shift, scale):
    sds = jax.ShapeDtypeStruct
    n_copies = 15 * 5 + 4
    shapes = [
        ((TOKENS, LANES), BF), ((TOKENS, LANES), BF), ((4, REACH, LANES), BF), ((4, REACH, LANES), BF), ((1536, SLAB), BF),
    ]
    return pl.pallas_call(
        functools.partial(row_forward_kernel, scale),
        out_shape=(
            sds((TOKENS, LANES), BF), *[sds(*shape) for shape in shapes], sds((96, SLAB), F32), sds((TOKENS, SLAB), F32),
        ),
        in_specs=[any_spec()] * 5 + [vmem_spec()] * 2,
        out_specs=(any_spec(),) * 6 + (vmem_spec(), any_spec()),
        scratch_shapes=[
            pltpu.VMEM((GROUP, 32, LANES), BF),
            pltpu.VMEM((GROUP, 48, SLAB), BF),
            pltpu.VMEM((3, LANES, LANES), BF),
            pltpu.VMEM((TOKENS, LANES), BF),
            pltpu.VMEM((SLAB, SLAB), F32),
            pltpu.VMEM((SLAB, SLAB), F32),
            pltpu.VMEM((1536, SLAB), F32),
            pltpu.VMEM((GROUP, 96, SLAB), F32),
            pltpu.VMEM((GROUP, 32, LANES), BF),
            *[pltpu.VMEM(*shape) for shape in shapes],
            pltpu.VMEM((TOKENS, SLAB), F32),
            pltpu.VMEM((8, LANES), F32),
            pltpu.SemaphoreType.DMA((n_copies,)),
            pltpu.SemaphoreType.DMA((n_copies,)),
            pltpu.SemaphoreType.DMA((5,)),
            pltpu.SemaphoreType.DMA((8,)),
        ],
        compiler_params=pltpu.CompilerParams(collective_id=1, has_side_effects=True, vmem_limit_bytes=60 * 2**20),
    )(x, aux, wq, wk, wv, row_gain, row_shift)


def row_backward_kernel(
    scale, dm, xrow_in, q_in, kx_in, vx_in, probs_in, gaps_in, wq_in, wk_in, wv_in, keep_in, give_in, *rest
):
    squares, rest = rest[:5], rest[5:]
    own, row_gain, row_shift, vectors, up_bias, rest = *rest[:5], rest[5:]
    back, *sums = rest[:10]
    small_out, rest = rest[10], rest[11:]
    (
        din, dmr, act_t, partial_p, arrived, grads_s, own_k, own_v, edge_out, edge_in, gq, gk, gv, grad_act, outgoing,
        weights, small, halves, slots, vecs, xrow, q, kx, vx, probs, gaps, row_weights,
        send_sem, recv_sem, local_sem, store_sem, *units,
    ) = rest
    spot = place()
    g = slab_place(spot)
    copies = Copies(send_sem, recv_sem)
    stores = Stores(store_sem)
    loads = [
        pltpu.make_async_copy(src, dst, local_sem.at[n])
        for n, (src, dst) in enumerate((
            (xrow_in, xrow), (dm.at[g], din.at[g]), (vx_in, vx), (probs_in, probs), (q_in, q), (kx_in, kx), (gaps_in, gaps),
            (wq_in, row_weights.at[0]), (wk_in, row_weights.at[1]), (wv_in, row_weights.at[2]),
        ))
    ]
    for copy in loads:
        copy.start()
    vector_rows(vecs, (row_gain, row_shift))
    gain, shift = vecs.at[0:1], vecs.at[1:2]
    greet(spot, slab_reach(spot)[:15] + [shifted(spot, "y", k) for k in (1, 2, 3)] + [shifted(spot, "aln", 1)])
    got = exchange(spot, copies, lambda i: dm.at[i], lambda me, k: din.at[me])

    def unit(n):
        if n == 5:
            give, keep = give_in, keep_in
        else:
            give, keep = squares[n].at[rows_of_half(1 - spot["aln"])], squares[n].at[rows_of_half(spot["aln"])]
        run = start_unit(spot, copies, units, n, give, keep, sums[n], BACK_ORDERS[n])
        run.step()
        return run

    first = [unit(n) for n in range(3)]
    loads[0].wait()

    def normed(k, carry):
        at = pl.ds(pl.multiple_of(128 * k, 128), 128)
        scaled, _ = centre(xrow[at, :].astype(F32))
        act_t[:, at] = jnp.transpose(scaled * gain[...] + shift[...]).astype(BF)
        return carry

    lax.fori_loop(0, 4, normed, 0)
    step_all(*first)
    loads[1].wait()
    wait_all(got)

    def regroup(k, carry):
        first = din[2 * k].astype(F32)
        second = din[2 * k + 1].astype(F32)
        for s in range(4):
            at = pl.ds(pl.multiple_of(SLAB * s + 16 * k, 16), 16)
            dmr[at, :] = jnp.concatenate([first[8 * s : 8 * s + 8], second[8 * s : 8 * s + 8]], axis=0).astype(BF)
        return carry

    lax.fori_loop(0, 8, regroup, 0)
    step_all(*first)
    second = [unit(n) for n in range(3, 6)]
    low_picks = quad_masks(BF)
    picks = quad_masks(F32)
    mine = pl.ds(pl.multiple_of(96 * g, 32), 96)
    loads[2].wait()

    def rows_of(s, b):
        return slice(SLAB * s + 64 * b, SLAB * s + 64 * b + 64)

    for b in range(2):
        for n in range(3):
            lanes = slice(256 * n, 256 * n + 256)
            total = None
            for s in range(4):
                term = dot_nt(spread_heads(dmr[rows_of(s, b), lanes], low_picks), vx[s, 64 * b : 64 * b + 128, lanes])
                total = term if total is None else total + term
            partial_p[256 * (3 * b + n) : 256 * (3 * b + n) + 256, :] = total.astype(BF)
    got = exchange(spot, copies, lambda i: partial_p.at[pl.ds(pl.multiple_of(96 * i, 32), 96)], lambda me, k: arrived.at[k])
    step_all(*first, *second)
    loads[3].wait()
    up, down = shifted(spot, "y", 1), shifted(spot, "y", -1)

    def scatter(weigh, source, target, which, factor):
        for n in range(3):
            lanes = slice(256 * n, 256 * n + 256)
            turned = [
                jnp.transpose(weigh[256 * (3 * b + n) : 256 * (3 * b + n) + 256, :].astype(F32)).astype(BF) for b in range(2)
            ]
            for s in range(4):
                first, second = [
                    dot_nn(turned[b], spread_heads(source[rows_of(s, b), lanes], low_picks)) * factor for b in range(2)
                ]
                edge_out[which, 0, s, :, lanes] = first[0:32].astype(BF)
                target[s, 0:32, lanes] = first[32:64]
                target[s, 32:96, lanes] = first[64:128] + second[0:64]
                target[s, 96:128, lanes] = second[64:96]
                edge_out[which, 1, s, :, lanes] = second[96:128].astype(BF)
        return [
            copies.start(edge_out.at[which, 0], edge_in.at[which, 0], down),
            copies.start(edge_out.at[which, 1], edge_in.at[which, 1], up),
        ]

    edges_v = scatter(probs, dmr, own_v, 0, 1.0)
    step_all(*first)
    wait_all(got)
    total = partial_p[mine, :].astype(F32)
    for k in range(1, GROUP):
        total = total + arrived[k].astype(F32)
    share = own[...]
    grads_s[mine, :] = (share * (total - jnp.sum(share * total, axis=-1, keepdims=True))).astype(BF)
    got = exchange(spot, copies, lambda i: grads_s.at[mine], lambda me, k: grads_s.at[mine])

    def collect(edges, which, source, target):
        wait_all(edges)
        for s in range(4):
            own_rows = source[s]
            first = own_rows[0:32] + edge_in[which, 1, s].astype(F32)
            last = own_rows[96:128] + edge_in[which, 0, s].astype(F32)
            joined = jnp.concatenate([first, own_rows[32:96], last], axis=0)
            if which == 1:
                weigh = gaps[SLAB * s : SLAB * s + SLAB, :]
                joined = joined * jnp.concatenate([weigh] * 6, axis=1)
            target[SLAB * s : SLAB * s + SLAB, :] = joined.astype(BF)

    def weight_unit(n, grad):
        for lanes in THIRDS:
            for at in THIRDS:
                weights[n, at, lanes] = dot_nn(act_t[at, :], grad[:, lanes]).astype(BF)
        scratch = [part.at[6 + n] for part in units[1:4]]
        run = Run(reduce_unit(
            spot, copies, lambda: None, weights.at[n, rows_of_half(1 - spot["aln"])], weights.at[n], spot["aln"] * HALF,
            *scratch, sums[6 + n], units[5].at[6 + n], ROW_ORDERS[n]))
        run.step()
        return run

    step_all(*first, *second)
    collect(edges_v, 0, own_v, gv)
    run_v = weight_unit(2, gv)
    for copy in loads[4:7]:
        copy.wait()
    wait_all(got)
    step_all(*first, *second)
    edges_k = scatter(grads_s, q, own_k, 1, scale)
    step_all(*first, *second, run_v)
    for b in range(2):
        for n, lanes in enumerate(THIRDS):
            weigh = grads_s[256 * (3 * b + n) : 256 * (3 * b + n) + 256, :]
            for s in range(4):
                made = gather_heads(dot_nn(weigh, kx[s, 64 * b : 64 * b + 128, lanes]), picks) * scale
                gq[rows_of(s, b), lanes] = (made * wide(gaps[rows_of(s, b), :])).astype(BF)
    run_q = weight_unit(0, gq)
    step_all(*first, *second, run_v)
    collect(edges_k, 1, own_k, gk)
    run_k = weight_unit(1, gk)
    for copy in loads[7:10]:
        copy.wait()
    step_all(*second, run_v, run_q)
    wq, wk, wv = [row_weights.at[n] for n in range(3)]
    for at in THIRDS:
        grad_act[:, at] = (
            dot_nt(gq[...], wq[at, :]) + dot_nt(gk[...], wk[at, :]) + dot_nt(gv[...], wv[at, :])
        )
    step_all(*first, *second, run_v, run_q, run_k)

    def norm_back(k, carry):
        grad_gain, grad_shift = carry
        made = []
        for s in range(4):
            at = pl.ds(pl.multiple_of(SLAB * s + 16 * k, 16), 16)
            scaled, inverse = centre(xrow[at, :].astype(F32))
            upstream = grad_act[at, :]
            product = upstream * scaled
            grad_gain = grad_gain + product[0:8] + product[8:16]
            grad_shift = grad_shift + upstream[0:8] + upstream[8:16]
            inner = upstream * gain[...]
            middle = inner - jnp.mean(inner, axis=-1, keepdims=True)
            middle = middle - scaled * jnp.mean(inner * scaled, axis=-1, keepdims=True)
            made.append(inverse * middle)
        for pair in range(2):
            for t in range(2):
                outgoing[2 * k + t, 16 * pair : 16 * pair + 16, :] = jnp.concatenate(
                    [m[8 * t : 8 * t + 8] for m in made[2 * pair : 2 * pair + 2]], axis=0
                ).astype(BF)
        return grad_gain, grad_shift

    zero = jnp.zeros((8, LANES), F32)
    grad_gain, grad_shift = lax.fori_loop(0, 8, norm_back, (zero, zero))
    at = pl.ds(pl.multiple_of(32 * g, 32), 32)
    got = exchange(spot, copies, lambda i: outgoing.at[i], lambda me, k: back.at[at])
    stores.start(outgoing.at[g], back.at[at])
    bias_rows = [
        jnp.concatenate([up_bias[:, HALF * j : HALF * j + HALF], up_bias[:, HALF * (j + 4) : HALF * (j + 5)]], axis=1)
        for j in range(4)
    ]
    sums_here = [jnp.sum(v, axis=0, keepdims=True) for v in (grad_gain, grad_shift)]
    small[...] = jnp.concatenate(
        sums_here + [vectors[0:5, :]] + bias_rows + [jnp.zeros((5, LANES), F32)], axis=0
    )
    finish_all(run_k, run_q, run_v, *second, *first, Run(sum_small(spot, copies, small, halves, slots)))
    wait_all(got)
    copies.finish()
    stores.finish()
    small_out[...] = halves[3]


BACK_ORDERS = (("y", "z", "x"), ("x", "y", "z"), ("z", "y", "x"), ("y", "x", "z"), ("y", "z", "x"), ("z", "y", "x"))
ROW_ORDERS = (("x", "y", "z"), ("z", "y", "x"), ("y", "x", "z"))


def rows_of_half(which):
    return pl.ds(pl.multiple_of(which * HALF, HALF), HALF)


def row_backward(dm, kept, wq, wk, wv, keep, give, squares, own, row_gain, row_shift, vectors, up_bias, scale):
    sds = jax.ShapeDtypeStruct
    n_copies = 15 * 4 + 4 + 9 * UNIT_COPIES + SMALL_COPIES
    low = pltpu.VMEM((TOKENS, LANES), BF)
    share = sds((HALF, LANES), BF)
    reach = pltpu.VMEM((4, REACH, LANES), BF)
    return pl.pallas_call(
        functools.partial(row_backward_kernel, scale),
        out_shape=(sds((TOKENS, LANES), BF), *[share] * 9, sds((16, HALF), F32)),
        in_specs=[any_spec()] * 17 + [vmem_spec()] * 5,
        out_specs=(any_spec(),) * 10 + (vmem_spec(),),
        scratch_shapes=[
            pltpu.VMEM((GROUP, 32, LANES), BF),
            low,
            pltpu.VMEM((LANES, TOKENS), BF),
            pltpu.VMEM((1536, SLAB), BF),
            pltpu.VMEM((GROUP, 96, SLAB), BF),
            pltpu.VMEM((1536, SLAB), BF),
            pltpu.VMEM((4, SLAB, LANES), F32),
            pltpu.VMEM((4, SLAB, LANES), F32),
            pltpu.VMEM((2, 2, 4, 32, LANES), BF),
            pltpu.VMEM((2, 2, 4, 32, LANES), BF),
            low,
            low,
            low,
            pltpu.VMEM((TOKENS, LANES), F32),
            pltpu.VMEM((GROUP, 32, LANES), BF),
            pltpu.VMEM((3, LANES, LANES), BF),
            pltpu.VMEM((16, LANES), F32),
            pltpu.VMEM((4, 16, HALF), F32),
            pltpu.VMEM((13, 16, HALF), F32),
            pltpu.VMEM((8, LANES), F32),
            low,
            low,
            reach,
            reach,
            pltpu.VMEM((1536, SLAB), BF),
            pltpu.VMEM((TOKENS, SLAB), F32),
            pltpu.VMEM((3, LANES, LANES), BF),
            pltpu.SemaphoreType.DMA((n_copies,)),
            pltpu.SemaphoreType.DMA((n_copies,)),
            pltpu.SemaphoreType.DMA((10,)),
            pltpu.SemaphoreType.DMA((1,)),
            *unit_scratch(9, 6),
        ],
        compiler_params=pltpu.CompilerParams(collective_id=2, has_side_effects=True, vmem_limit_bytes=60 * 2**20),
    )(dm, *kept, wq, wk, wv, keep, give, *squares, own, row_gain, row_shift, vectors, up_bias)


TOKENS = 512
TILE = 256
THIRDS = [slice(256 * n, 256 * n + 256) for n in range(3)]


def to_columns():
    row = lax.broadcasted_iota(jnp.int32, (TOKENS, TOKENS), 0)
    token = lax.broadcasted_iota(jnp.int32, (TOKENS, TOKENS), 1)
    want = lax.rem(row, 64) * 8 + lax.div(row, 64)
    return (token == want).astype(F32).astype(BF)


def to_sequences():
    row = lax.broadcasted_iota(jnp.int32, (TOKENS, TOKENS), 0)
    token = lax.broadcasted_iota(jnp.int32, (TOKENS, TOKENS), 1)
    want = lax.rem(row, 8) * 64 + lax.div(row, 8)
    return (token == want).astype(F32).astype(BF)


def rows_loop(count, body, init=0):
    def step(k, carry):
        return body(pl.ds(pl.multiple_of(64 * k, 64), 64), carry)

    return lax.fori_loop(0, count // 64, step, init)


def normed_rows(values, gain, shift, act, act_t):
    def body(k, carry):
        at = pl.ds(pl.multiple_of(128 * k, 128), 128)
        scaled, _ = centre(values[at, :])
        made = scaled * gain[...] + shift[...]
        act[at, :] = made.astype(BF)
        if act_t is not None:
            act_t[:, at] = jnp.transpose(made).astype(BF)
        return carry

    lax.fori_loop(0, TOKENS // 128, body, 0)


def norm_back_rows(values, upstream, gain, residual, out):
    def body(at, carry):
        grad_gain, grad_shift = carry
        scaled, inverse = centre(values[at, :])
        up = upstream[at, :]
        product = up * scaled
        for r in range(8):
            grad_gain = grad_gain + product[8 * r : 8 * r + 8]
            grad_shift = grad_shift + up[8 * r : 8 * r + 8]
        inner = up * gain[...]
        middle = inner - jnp.mean(inner, axis=-1, keepdims=True)
        middle = middle - scaled * jnp.mean(inner * scaled, axis=-1, keepdims=True)
        out[at, :] = residual[at, :].astype(F32) + inverse * middle
        return grad_gain, grad_shift

    zero = jnp.zeros((8, LANES), F32)
    return rows_loop(TOKENS, body, (zero, zero))


def column_probs(scale, queries, keys, at, lanes, picks):
    heads = spread_heads(queries[at, lanes], picks)
    scores = dot_nt(heads, keys[at, lanes]) * scale
    expo = jnp.exp(scores - jnp.max(scores, axis=-1, keepdims=True))
    return heads, expo / jnp.sum(expo, axis=-1, keepdims=True)


def column_kernel(
    scale, x, mixed, cot, wq, wk, wv, col_out, row_out, up, down,
    col_gain, col_shift, mlp_gain, mlp_shift, down_bias_in, up_bias_in,
    result_out, grad_inputs_out, grad_row_mixed_out, dwq_out, dwk_out, dwv_out, dw_col_out, dw_row_out, keep_out, give_out,
    sum_down, sum_up, vectors, grad_up_bias,
    squares, vecs, up_bias, weights, up_tiles, down_tiles, raw, order, mixed_cs, act, act_t, after_row, after_col, made, grad_act,
    queries, keys, values, col_mixed, cot_cs, keep_down, give_down, keep_up, give_up, swap, recv, pieces,
    load_sem, tile_sem, store_sem, out_sem, send_sem, recv_sem,
):
    spot = place()
    side = spot["aln"]
    copies = Copies(send_sem, recv_sem)
    stores = Stores(out_sem)
    vector_rows(vecs, (col_gain, col_shift, mlp_gain, mlp_shift, down_bias_in))
    up_bias[...] = up_bias_in[...].reshape(1, 4 * LANES)
    loads = [
        pltpu.make_async_copy(src, dst, load_sem.at[n])
        for n, (src, dst) in enumerate((
            (mixed, raw.at[1]), (x, raw.at[0]), (row_out, weights.at[4]), (wq, weights.at[0]), (wk, weights.at[1]),
            (wv, weights.at[2]), (col_out, weights.at[3]), (cot, raw.at[2]),
        ))
    ]
    for copy in loads:
        copy.start()
    steps = 2 * 2 * 3

    def spot_of(j):
        half = side if (j // 3) % 2 == 0 else 1 - side
        return half, pl.multiple_of(half * (4 * HALF) + (j // 6) * LANES + (j % 3) * TILE, TILE)

    def fetch(j):
        _, at = spot_of(j)
        slot = j % 3
        return [
            pltpu.make_async_copy(up.at[:, pl.ds(at, TILE)], up_tiles.at[slot], tile_sem.at[slot, 0]),
            pltpu.make_async_copy(down.at[pl.ds(at, TILE)], down_tiles.at[slot], tile_sem.at[slot, 1]),
        ]

    greet(spot, torus_reach(spot))
    order[...] = to_columns()
    loads[0].wait()
    for lanes in THIRDS:
        mixed_cs[:, lanes] = dot_nn(order[...], raw[1, :, lanes]).astype(BF)
    loads[1].wait()
    loads[2].wait()
    for lanes in THIRDS:
        after_row[:, lanes] = dot_nn(order[...], raw[0, :, lanes]) + dot_nn(mixed_cs[...], weights[4, :, lanes])
    normed_rows(after_row, vecs.at[0:1], vecs.at[1:2], act, None)
    for j in range(2):
        for copy in fetch(j):
            copy.start()
    for n, out in enumerate((queries, keys, values)):
        loads[3 + n].wait()
        for lanes in THIRDS:
            out[:, lanes] = dot_nn(act[...], weights[n, :, lanes]).astype(BF)
    low_picks, picks = quad_masks(BF), quad_masks(F32)

    def attend(at, carry):
        for lanes in THIRDS:
            _, probs = column_probs(scale, queries, keys, at, lanes, low_picks)
            mixes = dot_nn(probs.astype(BF), values[at, lanes])
            col_mixed[at, lanes] = gather_heads(mixes, picks).astype(BF)
        return carry

    rows_loop(TOKENS, attend)
    loads[6].wait()
    for lanes in THIRDS:
        after_col[:, lanes] = after_row[:, lanes] + dot_nn(col_mixed[...], weights[3, :, lanes])
    gain, shift, down_bias = vecs.at[2:3], vecs.at[3:4], vecs.at[4:5]
    normed_rows(after_col, gain, shift, act, act_t)
    loads[7].wait()
    for lanes in THIRDS:
        cot_cs[:, lanes] = dot_nn(order[...], raw[2, :, lanes]).astype(BF)
    order[...] = to_sequences()

    def down_unit(n):
        at = HALF * n
        run = Run(reduce_unit(
            spot, copies, lambda: None, give_down.at[at : at + HALF], keep_down, at, swap.at[n], recv.at[n], pieces.at[n],
            sum_down.at[at : at + HALF], store_sem.at[n], DOWN_ORDERS[n]))
        run.step()
        return run

    def up_unit(k):
        n = 3 + k
        run = Run(reduce_unit(
            spot, copies, lambda: None, give_up.at[k], keep_up.at[k], 0, swap.at[n], recv.at[n], pieces.at[n],
            sum_up.at[:, LANES * k : LANES * k + LANES], store_sem.at[n], UP_ORDERS[k]))
        run.step()
        return run

    for j in range(steps):
        half, at = spot_of(j)
        slot, i = j % 3, j // 6
        if j + 2 < steps:
            for copy in fetch(j + 2):
                copy.start()
        for copy in fetch(j):
            copy.wait()
        hidden_pre = dot_nn(act[...], up_tiles[slot]) + up_bias[:, pl.ds(at, TILE)]
        grad_hidden = dot_nt(cot_cs[...], down_tiles[slot])
        phi = 0.5 + 0.5 * lax.erf(hidden_pre * (1.0 / math.sqrt(2.0)))
        slope = phi + hidden_pre * jnp.exp(-0.5 * hidden_pre * hidden_pre) * (1.0 / math.sqrt(2.0 * math.pi))
        hidden = (hidden_pre * phi).astype(BF)
        pre = (grad_hidden * slope).astype(BF)
        tall = keep_down if (j // 3) % 2 == 0 else give_down
        rows = slice(LANES * i + TILE * (j % 3), LANES * i + TILE * (j % 3) + TILE)
        lanes_here = slice(TILE * (j % 3), TILE * (j % 3) + TILE)
        k = 2 * half + i
        for lanes in THIRDS:
            if j == 0:
                made[:, lanes] = dot_nn(hidden, down_tiles[slot, :, lanes])
                grad_act[:, lanes] = dot_nt(pre, up_tiles[slot, lanes, :])
            else:
                made[:, lanes] += dot_nn(hidden, down_tiles[slot, :, lanes])
                grad_act[:, lanes] += dot_nt(pre, up_tiles[slot, lanes, :])
            tall[rows, lanes] = dot_tn(hidden, cot_cs[:, lanes]).astype(BF)
        for which, out in ((side, keep_up), (1 - side, give_up)):
            out[k, :, lanes_here] = dot_nn(act_t[rows_of_half(which), :], pre).astype(BF)
        grad_up_bias[:, pl.ds(at, TILE)] = jnp.sum(pre.astype(F32), axis=0, keepdims=True)
        if j == 5:
            first = [down_unit(0), up_unit(0), up_unit(2)]
        if j == 7:
            step_all(*first)
            late = down_unit(1)
        if j == 9:
            step_all(*first, late)
        if j == 11:
            step_all(*first, late)
            second = [down_unit(2), up_unit(1), up_unit(3)]
    stores.start(keep_down.at[3 * HALF : 4 * HALF], keep_out)
    stores.start(give_down.at[3 * HALF : 4 * HALF], give_out)
    for lanes in THIRDS:
        full = after_col[:, lanes] + (made[:, lanes] + down_bias[:, lanes])
        raw[2, :, lanes] = dot_nn(order[...], full.astype(BF)).astype(BF)
    stores.start(raw.at[2], result_out)
    sum_gain, sum_shift = norm_back_rows(after_col, grad_act, gain, cot_cs, after_col)

    def bias_sum(at, carry):
        values_here = cot_cs[at, :].astype(F32)
        for r in range(8):
            carry = carry + values_here[8 * r : 8 * r + 8]
        return carry

    bias = rows_loop(TOKENS, bias_sum, jnp.zeros((8, LANES), F32))
    branch, grad_mixed = raw.at[0], raw.at[1]

    def rounded(at, carry):
        branch[at, :] = after_col[at, :].astype(BF)
        return carry

    rows_loop(TOKENS, rounded)
    step_all(*first, late, *second)
    for lanes in THIRDS:
        grad_mixed[:, lanes] = dot_nt(branch[...], weights[3, lanes, :]).astype(BF)
    gain, shift = vecs.at[0:1], vecs.at[1:2]
    normed_rows(after_row, gain, shift, act, act_t)

    def attend_back(k, carry):
        at = pl.ds(pl.multiple_of(64 * k, 64), 64)
        for lanes in THIRDS:
            heads, probs = column_probs(scale, queries, keys, at, lanes, low_picks)
            upstream = spread_heads(grad_mixed[at, lanes], low_picks)
            grad_probs = dot_nt(upstream, values[at, lanes])
            grad_scores = probs * (grad_probs - jnp.sum(probs * grad_probs, axis=-1, keepdims=True))
            grad_scores = grad_scores.astype(BF)
            gq = (gather_heads(dot_nn(grad_scores, keys[at, lanes]), picks) * scale).astype(BF)
            gk = (dot_tn(grad_scores, heads) * scale).astype(BF)
            gv = dot_tn(probs.astype(BF), upstream).astype(BF)
            queries[at, lanes] = gq
            keys[at, lanes] = gk
            values[at, lanes] = gv
        return carry

    for n, runs in enumerate(((*first, late, *second), (late,), (*first, *second), (late,))):
        lax.fori_loop(2 * n, 2 * n + 2, attend_back, 0)
        step_all(*runs)
    for lanes in THIRDS:
        grad_act[:, lanes] = (
            dot_nt(queries[...], weights[0, lanes, :])
            + dot_nt(keys[...], weights[1, lanes, :])
            + dot_nt(values[...], weights[2, lanes, :])
        )
    for at in THIRDS:
        squares[0, at, :] = dot_tn(col_mixed[:, at], branch[...]).astype(BF)
    stores.start(squares.at[0], dw_col_out)
    step_all(*first, *second)
    grad_gain, grad_shift = norm_back_rows(after_row, grad_act, gain, after_col, after_row)
    sums = [jnp.sum(v, axis=0, keepdims=True) for v in (grad_gain, grad_shift, sum_gain, sum_shift, bias)]
    vectors[...] = jnp.concatenate(sums + [jnp.zeros((3, LANES), F32)], axis=0)

    def rounded_row(at, carry):
        values_here = after_row[at, :]
        high = values_here.astype(BF)
        branch[at, :] = high
        act[at, :] = (values_here - high.astype(F32)).astype(BF)
        return carry

    rows_loop(TOKENS, rounded_row)
    for lanes in THIRDS:
        grad_mixed[:, lanes] = dot_nt(branch[...], weights[4, lanes, :]).astype(BF)
    for lanes in THIRDS:
        cot_cs[:, lanes] = dot_nn(order[...], grad_mixed[:, lanes]).astype(BF)
        made[:, lanes] = dot_nn(order[...], branch[:, lanes]) + dot_nn(order[...], act[:, lanes])
    stores.start(cot_cs, grad_row_mixed_out)
    stores.start(made, grad_inputs_out)
    step_all(*first, late, *second)
    for n, (grad, out) in enumerate(((queries, dwq_out), (keys, dwk_out), (values, dwv_out))):
        for at in THIRDS:
            squares[1 + n, at, :] = dot_nn(act_t[at, :], grad[...]).astype(BF)
        stores.start(squares.at[1 + n], out)
        if n == 1:
            step_all(late, *second)
    for at in THIRDS:
        squares[4, at, :] = dot_tn(mixed_cs[:, at], branch[...]).astype(BF)
    stores.start(squares.at[4], dw_row_out)
    finish_all(*first, late, *second)
    copies.finish()
    stores.finish()


DOWN_ORDERS = (("y", "z", "x"), ("y", "x", "z"), ("y", "z", "x"))
UP_ORDERS = (("x", "y", "z"), ("x", "z", "y"), ("z", "x", "y"), ("z", "y", "x"))


def column_part(
    x, mixed, cot, wq, wk, wv, col_out, row_out, up, down, col_gain, col_shift, mlp_gain, mlp_shift, down_bias, up_bias, scale
):
    sds = jax.ShapeDtypeStruct
    hidden = up.shape[1]
    square, share, tokens = sds((LANES, LANES), BF), sds((HALF, LANES), BF), sds((TOKENS, LANES), BF)
    low = pltpu.VMEM((TOKENS, LANES), BF)
    full = pltpu.VMEM((TOKENS, LANES), F32)
    n_copies = 7 * UNIT_COPIES
    return pl.pallas_call(
        functools.partial(column_kernel, scale),
        out_shape=(
            tokens, sds((TOKENS, LANES), F32), tokens, square, square, square, square, square, share, share,
            sds((3 * HALF, LANES), BF), sds((HALF, hidden), BF), sds((8, LANES), F32), sds((1, hidden), F32),
        ),
        in_specs=[any_spec()] * 10 + [vmem_spec()] * 6,
        out_specs=(any_spec(),) * 12 + (vmem_spec(),) * 2,
        scratch_shapes=[
            pltpu.VMEM((5, LANES, LANES), BF),
            pltpu.VMEM((8, LANES), F32),
            pltpu.VMEM((1, hidden), F32),
            pltpu.VMEM((5, LANES, LANES), BF),
            pltpu.VMEM((3, LANES, TILE), BF),
            pltpu.VMEM((3, TILE, LANES), BF),
            pltpu.VMEM((3, TOKENS, LANES), BF),
            pltpu.VMEM((TOKENS, TOKENS), BF),
            low, low, pltpu.VMEM((LANES, TOKENS), BF), full, full, full, full, low, low, low, low, low,
            pltpu.VMEM((hidden // 2, LANES), BF),
            pltpu.VMEM((hidden // 2, LANES), BF),
            pltpu.VMEM((4, HALF, LANES), BF),
            pltpu.VMEM((4, HALF, LANES), BF),
            pltpu.VMEM((7, HALF, LANES), BF),
            pltpu.VMEM((7, 3 * QUARTER, LANES), BF),
            pltpu.VMEM((7, 7, PIECE, HALF), BF),
            pltpu.SemaphoreType.DMA((8,)),
            pltpu.SemaphoreType.DMA((3, 2)),
            pltpu.SemaphoreType.DMA((7,)),
            pltpu.SemaphoreType.DMA((10,)),
            pltpu.SemaphoreType.DMA((n_copies,)),
            pltpu.SemaphoreType.DMA((n_copies,)),
        ],
        compiler_params=pltpu.CompilerParams(collective_id=3, has_side_effects=True, vmem_limit_bytes=60 * 2**20),
    )(
        x, mixed, cot, wq, wk, wv, col_out, row_out, up, down,
        col_gain, col_shift, mlp_gain, mlp_shift, down_bias, up_bias,
    )


def finish_kernel(n, *refs):
    base, back, *shares = refs[: n + 2]
    most, last, total, *outs, joined = refs[n + 2 :]
    total[...] = base[...] + back[...].astype(F32)
    for share, out in zip(shares, outs):
        out[...] = share[...].astype(F32)
    step = pl.program_id(0)

    @pl.when(step < 6)
    def _():
        joined[...] = most[...].astype(F32)

    @pl.when(step >= 6)
    def _():
        joined[...] = last[...].astype(F32)


def finish(base, back, shares, most, last):
    steps = 8
    arrays = [base, back, *shares]
    specs = [pl.BlockSpec((a.shape[0] // steps, a.shape[1]), lambda i: (i, 0)) for a in arrays]
    part = (most.shape[0] // 6, most.shape[1])
    ends = [
        pl.BlockSpec(part, lambda i: (jnp.minimum(i, 5), 0)),
        pl.BlockSpec(part, lambda i: (jnp.maximum(i - 6, 0), 0)),
    ]
    sds = jax.ShapeDtypeStruct
    return pl.pallas_call(
        functools.partial(finish_kernel, len(shares)),
        grid=(steps,),
        out_shape=[sds(a.shape, F32) for a in (base, *shares)] + [sds((part[0] * steps, part[1]), F32)],
        in_specs=specs + ends,
        out_specs=[specs[0]] + specs[2:] + [pl.BlockSpec(part, lambda i: (i, 0))],
        compiler_params=pltpu.CompilerParams(vmem_limit_bytes=40 * 2**20),
    )(*arrays, most, last)


def side_inputs(gap_flags, band_mask):
    col = lax.axis_index("col")
    weights = (1.0 - GAP_DROP * gap_flags.astype(F32)).reshape(GROUP, 32, 1)
    query = 8 * lax.rem(col, 8) + jnp.arange(8, dtype=jnp.int32)[:, None]
    key = jnp.arange(SLAB, dtype=jnp.int32)[None, :]
    offset = key - query
    chosen = (offset[:, :, None] == jnp.arange(2 * BAND + 1, dtype=jnp.int32)) & (band_mask[:, None, :] == 1)
    where = 64 * lax.div(col, 8) + key - BAND
    allowed = (jnp.any(chosen, axis=-1) | (offset == BAND)) & (where >= 0) & (where < COLS)
    allowed = jnp.broadcast_to(allowed.astype(F32)[None], (GROUP, 8, SLAB))
    weights = jnp.broadcast_to(weights, (GROUP, 32, SLAB))
    return jnp.concatenate([weights, allowed, jnp.zeros((GROUP, 8, SLAB), F32)], axis=1).astype(BF)


def per_device(
    inputs,
    gap_flags,
    band_mask,
    row_gain,
    row_shift,
    row_query,
    row_key,
    row_value,
    row_out,
    col_gain,
    col_shift,
    col_query,
    col_key,
    col_value,
    col_out,
    mlp_gain,
    mlp_shift,
    mlp_up,
    up_bias,
    mlp_down,
    down_bias,
    cotangent,
):
    seqs, width_cols, model = (inputs.shape[1], inputs.shape[2], inputs.shape[3])
    low_tokens = (seqs * width_cols, model)
    row_scale = 1.0 / math.sqrt(HD * seqs)
    col_scale = 1.0 / math.sqrt(HD)
    aux = side_inputs(gap_flags[0], band_mask[0])
    mixed_low, *kept_row, own, gaps = row_forward(
        inputs.reshape(GROUP, 32, model), aux, row_query, row_key, row_value, row_gain, row_shift, row_scale
    )
    (
        result, grad_after_row, grad_row_mixed, grad_cq, grad_ck, grad_cv, grad_co, grad_ro, keep, give,
        sum_down, sum_up, vectors, grad_up_bias,
    ) = column_part(
        inputs.reshape(low_tokens), mixed_low, cotangent.reshape(low_tokens), col_query, col_key, col_value, col_out,
        row_out, mlp_up, mlp_down, col_gain, col_shift, mlp_gain, mlp_shift, down_bias, up_bias, col_scale,
    )
    back_row, sum_co, sum_cq, sum_ck, sum_cv, sum_ro, last_down, sum_rq, sum_rk, sum_rv, small_sum = row_backward(
        grad_row_mixed.reshape(GROUP, 32, model), (*kept_row, gaps), row_query, row_key, row_value, keep, give,
        (grad_co, grad_cq, grad_ck, grad_cv, grad_ro), own, row_gain, row_shift, vectors, grad_up_bias, row_scale,
    )
    grad_inputs, *sums = finish(
        grad_after_row, back_row,
        [sum_rq, sum_rk, sum_rv, sum_ro, sum_cq, sum_ck, sum_cv, sum_co, sum_up], sum_down, last_down,
    )
    return (
        result.reshape(inputs.shape),
        grad_inputs.reshape(inputs.shape),
        small_sum[0],
        small_sum[1],
        *sums[0:4],
        small_sum[2],
        small_sum[3],
        *sums[4:8],
        small_sum[4],
        small_sum[5],
        sums[8],
        small_sum[7:11].reshape(4 * HALF),
        sums[9],
        small_sum[6],
    )


def solution(mesh):
    in_specs = (
        P("aln", None, "col", None),
        P("aln", None, "col"),
        P("aln", "col", None),
        P(),
        P(),
        P(),
        P(),
        P(),
        P(),
        P(),
        P(),
        P(),
        P(),
        P(),
        P(),
        P(),
        P(),
        P(),
        P(),
        P(),
        P(),
        P("aln", None, "col", None),
    )
    out_specs = (
        P("aln", None, "col", None),
        P("aln", None, "col", None),
        P("aln"),
        P("aln"),
        P("aln", None),
        P("aln", None),
        P("aln", None),
        P("aln", None),
        P("aln"),
        P("aln"),
        P("aln", None),
        P("aln", None),
        P("aln", None),
        P("aln", None),
        P("aln"),
        P("aln"),
        P("aln", None),
        P("aln"),
        P("aln", None),
        P("aln"),
    )
    return jax.shard_map(
        per_device, mesh=mesh, in_specs=in_specs, out_specs=out_specs, check_vma=False
    )
```

```python
import functools
import math

import jax
import jax.numpy as jnp
from jax import lax
from jax.experimental import pallas as pl
from jax.experimental.pallas import tpu as pltpu
from jax.sharding import PartitionSpec as P

H = 12
HD = 64
COLS = 512
BAND = 32


GAP_DROP = 0.75
MESH = pl.DeviceIdType.MESH
LANES = 768
HALF = 384
THIRD = 128
QUARTER = 32
PIECE = 16
BF = jnp.bfloat16
F32 = jnp.float32


def place():
    col = lax.axis_index("col")
    return {
        "aln": lax.axis_index("aln"),
        "x": lax.rem(col, 4),
        "z": lax.rem(lax.div(col, 4), 4),
        "y": lax.div(col, 16),
    }


def device_at(spot):
    return (spot["aln"], spot["y"] * 16 + spot["z"] * 4 + spot["x"])


def mod4(v):
    return lax.rem(v + 4, 4)


def shifted(spot, axis, step):
    if axis == "aln":
        return device_at({**spot, "aln": 1 - spot["aln"]})
    return device_at({**spot, axis: mod4(spot[axis] + step)})


def greet(spot, reach):
    barrier = pltpu.get_barrier_semaphore()
    for peer in reach:
        pl.semaphore_signal(barrier, inc=1, device_id=peer, device_id_type=MESH)
    pl.semaphore_wait(barrier, len(reach))


def torus_reach(spot):
    return [shifted(spot, a, s) for a in "xyz" for s in (1, 2, 3)] + [shifted(spot, "aln", 1)]


def block(rows, count, lanes=0, width=LANES):
    return (slice(None), pl.ds(pl.multiple_of(rows, 16), count), pl.ds(pl.multiple_of(lanes, 128), width))


def add_into(dst, at, sources):
    total = dst[at]
    for ref, near in sources:
        total = total + ref[near]
    dst[at] = total


class Copies:
    def __init__(self, send_sem, recv_sem):
        self.send_sem, self.recv_sem, self.used, self.sent = send_sem, recv_sem, 0, []

    def start(self, src, dst, device):
        k = self.used
        self.used += 1
        copy = pltpu.make_async_remote_copy(
            src_ref=src, dst_ref=dst, send_sem=self.send_sem.at[k], recv_sem=self.recv_sem.at[k],
            device_id=device, device_id_type=MESH)
        copy.start()
        self.sent.append(copy)
        return copy

    def finish(self):
        for copy in self.sent:
            copy.wait_send()
        self.sent = []


def wait_all(started):
    for copy in started:
        copy.wait_recv()


GROUP_COPIES = 60


def reduce_third(spot, copies, load, give, total, base, swap, recv, pieces, out, row, store_sem, order):
    first, second, third = order
    if load is not None:
        load.start()
    got = copies.start(give, swap, shifted(spot, "aln", 1))
    yield
    if load is not None:
        load.wait()
    got.wait_recv()
    for r in range(4):
        add_into(total, block(base + QUARTER * r, QUARTER), [(swap, block(QUARTER * r, QUARTER))])
    m = spot[first]
    up, down = shifted(spot, first, 1), shifted(spot, first, -1)

    def chunk(k, lane):
        return block(base + mod4(k) * QUARTER, QUARTER, lane, HALF)

    def slot(j):
        return block(QUARTER * (j % 3), QUARTER, HALF * (j // 3), HALF)

    relay_up = copies.start(total.at[chunk(m + 2, 0)], recv.at[slot(0)], up)
    relay_down = copies.start(total.at[chunk(m + 2, HALF)], recv.at[slot(3)], down)
    early_up = copies.start(total.at[chunk(m + 1, HALF)], recv.at[slot(1)], up)
    early_down = copies.start(total.at[chunk(m - 1, 0)], recv.at[slot(4)], down)
    yield
    relay_up.wait_recv()
    add_into(total, chunk(m + 1, 0), [(recv, slot(0))])
    late_up = copies.start(total.at[chunk(m + 1, 0)], recv.at[slot(2)], up)
    relay_down.wait_recv()
    add_into(total, chunk(m - 1, HALF), [(recv, slot(3))])
    late_down = copies.start(total.at[chunk(m - 1, HALF)], recv.at[slot(5)], down)
    yield
    wait_all([early_up, early_down, late_up, late_down])
    add_into(total, chunk(m, 0), [(recv, slot(2)), (recv, slot(4))])
    add_into(total, chunk(m, HALF), [(recv, slot(1)), (recv, slot(5))])
    n = spot[second]

    def piece(k, start):
        return block(start + m * QUARTER + lax.div(mod4(k), 2) * PIECE, PIECE, lax.rem(mod4(k), 2) * HALF, HALF)

    got = [copies.start(total.at[piece(n + d, base)], pieces.at[d - 1], shifted(spot, second, d)) for d in (1, 3, 2)]
    yield
    wait_all(got)
    own = total[piece(n, base)].astype(F32)
    for d in range(3):
        own = own + pieces[d].astype(F32)
    spread = spot[third]
    pieces[3 + spread] = own.astype(BF)
    got = [copies.start(pieces.at[3 + spread], pieces.at[3 + spread], shifted(spot, third, d)) for d in (1, 3, 2)]
    yield
    wait_all(got)
    own = pieces[3].astype(F32)
    for d in range(1, 4):
        own = own + pieces[3 + d].astype(F32)
    total[piece(n, base)] = own.astype(BF)
    store = pltpu.make_async_copy(total.at[piece(n, base)], out.at[piece(n, row)], store_sem)
    store.start()
    got = [copies.start(total.at[piece(n, base)], out.at[piece(n, row)], shifted(spot, second, d)) for d in (1, 3, 2)]
    yield
    store.wait()
    wait_all(got)

    def whole(k, lane=0, width=LANES):
        return out.at[block(row + mod4(k) * QUARTER, QUARTER, lane, width)]

    go_up = copies.start(whole(m), whole(m), up)
    go_down = copies.start(whole(m), whole(m), down)
    yield
    go_up.wait_recv()
    on_up = copies.start(whole(m - 1, 0, HALF), whole(m - 1, 0, HALF), up)
    go_down.wait_recv()
    on_down = copies.start(whole(m + 1, HALF, HALF), whole(m + 1, HALF, HALF), down)
    yield
    wait_all([on_up, on_down])


def sum_small(spot, copies, small, halves, slots):
    mine, other = spot["aln"], 1 - spot["aln"]

    def half(which):
        return (slice(None), pl.ds(pl.multiple_of(which * HALF, HALF), HALF))

    swap = copies.start(small.at[half(other)], slots.at[12], shifted(spot, "aln", 1))
    yield
    swap.wait_recv()
    halves[0] = small[half(mine)] + slots[12]
    for n, axis in enumerate(("x", "y", "z")):
        m = spot[axis]
        slots[4 * n + m] = halves[n]
        got = [copies.start(slots.at[4 * n + m], slots.at[4 * n + m], shifted(spot, axis, k)) for k in (1, 2, 3)]
        yield
        wait_all(got)
        halves[n + 1] = (slots[4 * n] + slots[4 * n + 1]) + (slots[4 * n + 2] + slots[4 * n + 3])


SMALL_COPIES = 10


class Run:
    def __init__(self, steps):
        self.steps, self.live = steps, True

    def step(self):
        if self.live:
            self.live = next(self.steps, "end") != "end"


def step_all(*runs):
    for run in runs:
        run.step()


def finish_all(*runs):
    while any(run.live for run in runs):
        step_all(*runs)


def vector_rows(scratch, vectors):
    for n, vector in enumerate(vectors):
        scratch[n : n + 1, :] = vector[...].reshape(1, LANES)


class Stores:
    def __init__(self, sems):
        self.sems, self.copies = sems, []

    def start(self, src, dst):
        copy = pltpu.make_async_copy(src, dst, self.sems.at[len(self.copies)])
        copy.start()
        self.copies.append(copy)
        return copy

    def finish(self):
        for copy in self.copies:
            copy.wait()


def group_scratch(n):
    return [
        pltpu.VMEM((n, HALF, LANES), BF),
        pltpu.VMEM((3, n, 3 * QUARTER, LANES), BF),
        pltpu.VMEM((3, 7, n, PIECE, HALF), BF),
        pltpu.SemaphoreType.DMA((3,)),
        pltpu.SemaphoreType.DMA((3,)),
    ]


def start_group(spot, copies, scratch, source, total, base, out, orders):
    swap, recv, pieces, load_sem, store_sem = scratch
    other, side = 1 - spot["aln"], spot["aln"]
    runs = []
    for t in range(3):
        rows = slice(THIRD * t, THIRD * t + THIRD)
        if isinstance(source, tuple):
            give, load, start = source[1].at[:, rows], None, THIRD * t
        else:
            give = source.at[:, pl.ds(pl.multiple_of(other * HALF + THIRD * t, THIRD), THIRD)]
            if base is None:
                keep = source.at[:, pl.ds(pl.multiple_of(side * HALF + THIRD * t, THIRD), THIRD)]
                load, start = pltpu.make_async_copy(keep, total.at[:, rows], load_sem.at[t]), THIRD * t
            else:
                load, start = None, base + THIRD * t
        runs.append(Run(reduce_third(
            spot, copies, load, give, total, start, swap.at[:, rows], recv.at[t], pieces.at[t], out, THIRD * t,
            store_sem.at[t], orders[t])))
    step_all(*runs)
    return runs


GROUP = 16
SLAB = 128
REACH = 192
EPSILON = 1e-05
NEG_FILL = -1000000000.0


def dot_nn(a, b):
    return lax.dot_general(a, b, (((1,), (0,)), ((), ())), preferred_element_type=F32)


def dot_nt(a, b):
    return lax.dot_general(a, b, (((1,), (1,)), ((), ())), preferred_element_type=F32)


def dot_tn(a, b):
    return lax.dot_general(a, b, (((0,), (0,)), ((), ())), preferred_element_type=F32)


def quad_masks(dtype):
    lane = lax.broadcasted_iota(jnp.int32, (1, 256), 1)
    return [((lane >= 64 * h) & (lane < 64 * h + 64)).astype(F32).astype(dtype) for h in range(4)]


def spread_heads(block, masks):
    return jnp.concatenate([block * m for m in masks], axis=0)


def gather_heads(block, masks):
    n = block.shape[0] // 4
    out = block[0:n] * masks[0]
    for h in range(1, 4):
        out = out + block[n * h : n * h + n] * masks[h]
    return out


SLAB_ORDER = (1, 4, 3, 12, 2, 8, 5, 7, 13, 15, 6, 9, 11, 14, 10)


def slab_place(spot):
    return spot["z"] * 4 + spot["x"]


def slab_peer(spot, k):
    dz, dx = k // 4, k % 4
    there = {**spot, "z": mod4(spot["z"] + dz), "x": mod4(spot["x"] + dx)}
    return device_at(there), slab_place(there)


def exchange(spot, copies, src_of, dst_of):
    out = []
    for k in SLAB_ORDER:
        device, index = slab_peer(spot, k)
        out.append(copies.start(src_of(index), dst_of(slab_place(spot), k), device))
    return out


def slab_reach(spot):
    return [slab_peer(spot, k)[0] for k in range(1, GROUP)] + [shifted(spot, "y", 1), shifted(spot, "y", -1)]


def centre(rows):
    center = rows - jnp.mean(rows, axis=-1, keepdims=True)
    inverse = lax.rsqrt(jnp.mean(center * center, axis=-1, keepdims=True) + EPSILON)
    return center * inverse, inverse


def wide(weights):
    return jnp.concatenate([weights, weights], axis=1)


def row_forward_kernel(
    scale, x, aux, wq, wk, wv, row_gain, row_shift,
    mixed, xrow_out, q_out, kx_out, vx_out, probs_out, own, gaps_out,
    xin, auxin, weights, act, masks_in, mask_pick, scores, arrived, outgoing, xrow, q, kx, vx, probs, gaps, vecs,
    send_sem, recv_sem, local_sem, store_sem,
):
    spot = place()
    g = slab_place(spot)
    copies = Copies(send_sem, recv_sem)
    stores = Stores(store_sem)
    locals_ = [
        pltpu.make_async_copy(aux.at[g], auxin.at[g], local_sem.at[0]),
        pltpu.make_async_copy(x.at[g], xin.at[g], local_sem.at[1]),
        pltpu.make_async_copy(wk, weights.at[0], local_sem.at[2]),
        pltpu.make_async_copy(wv, weights.at[1], local_sem.at[3]),
        pltpu.make_async_copy(wq, weights.at[2], local_sem.at[4]),
    ]
    for copy in locals_:
        copy.start()
    vector_rows(vecs, (row_gain, row_shift))
    gain, shift = vecs.at[0:1], vecs.at[1:2]
    greet(spot, slab_reach(spot))
    got = exchange(spot, copies, lambda i: x.at[i], lambda me, k: xin.at[me])
    got_aux = exchange(spot, copies, lambda i: aux.at[i], lambda me, k: auxin.at[me])
    locals_[0].wait()
    locals_[1].wait()

    def regroup_row(row):
        def body(h, carry):
            k = 2 * row + h
            first = xin[2 * k].astype(F32)
            second = xin[2 * k + 1].astype(F32)
            side = auxin[2 * k].astype(F32)
            other = auxin[2 * k + 1].astype(F32)
            for s in range(4):
                rows = jnp.concatenate([first[8 * s : 8 * s + 8], second[8 * s : 8 * s + 8]], axis=0)
                at = pl.ds(pl.multiple_of(SLAB * s + 16 * k, 16), 16)
                xrow[at, :] = rows.astype(BF)
                scaled, _ = centre(rows)
                act[at, :] = (scaled * gain[...] + shift[...]).astype(BF)
                gaps[at, :] = jnp.concatenate([side[8 * s : 8 * s + 8], other[8 * s : 8 * s + 8]], axis=0)
            at = pl.ds(pl.multiple_of(16 * k, 16), 16)
            masks_in[at, :] = jnp.concatenate([side[32:40], other[32:40]], axis=0)
            return carry

        lax.fori_loop(0, 2, body, 0)

    by_step = dict(zip(SLAB_ORDER, zip(got, got_aux)))
    for dz in (0, 3, 1, 2):
        for dx in range(4):
            if 4 * dz + dx > 0:
                wait_all(by_step[4 * dz + dx])
        regroup_row(mod4(spot["z"] - dz))
    stores.start(xrow, xrow_out)
    stores.start(gaps, gaps_out)
    halos = []
    up, down = shifted(spot, "y", 1), shifted(spot, "y", -1)

    def project(which):
        target = (kx, vx)[which]
        locals_[2 + which].wait()
        for lanes in THIRDS:
            made = dot_nn(act[...], weights[which, :, lanes])
            if which == 0:
                made = made * wide(gaps[...])
            for s in range(4):
                target[s, 32:160, lanes] = made[SLAB * s : SLAB * s + SLAB].astype(BF)
        halos.append([
            copies.start(target.at[:, 128:160], target.at[:, 0:32], up),
            copies.start(target.at[:, 32:64], target.at[:, 160:192], down),
        ])

    project(0)
    locals_[4].wait()
    for lanes in THIRDS:
        q[:, lanes] = (dot_nn(act[...], weights[2, :, lanes]) * wide(gaps[...])).astype(BF)
    stores.start(q, q_out)
    wait_all(halos[0])
    stores.start(kx, kx_out)
    picks = quad_masks(BF)
    for b in range(2):
        for n in range(3):
            lanes = THIRDS[n]
            total = None
            for s in range(4):
                heads = spread_heads(q[SLAB * s + 64 * b : SLAB * s + 64 * b + 64, lanes], picks)
                term = dot_nt(heads, kx[s, 64 * b : 64 * b + 128, lanes])
                total = term if total is None else total + term
            scores[256 * (3 * b + n) : 256 * (3 * b + n) + 256, :] = total
    got = exchange(spot, copies, lambda i: scores.at[pl.ds(pl.multiple_of(96 * i, 32), 96)], lambda me, k: arrived.at[k])
    project(1)
    rows = masks_in[pl.ds(pl.multiple_of(64 * lax.div(g, 8), 64), 64), :]
    mask_pick[0:64, :] = rows
    mask_pick[64:128, :] = rows
    allowed = mask_pick[pl.ds(pl.multiple_of(32 * lax.rem(g, 2), 32), 96), :]
    wait_all(got)
    mine = pl.ds(pl.multiple_of(96 * g, 32), 96)
    total = scores[mine, :]
    for k in range(1, GROUP):
        total = total + arrived[k]
    total = jnp.where(allowed > 0.5, total * scale, NEG_FILL)
    expo = jnp.exp(total - jnp.max(total, axis=-1, keepdims=True))
    share = expo / jnp.sum(expo, axis=-1, keepdims=True)
    probs[mine, :] = share.astype(BF)
    got = exchange(spot, copies, lambda i: probs.at[mine], lambda me, k: probs.at[mine])
    own[...] = share
    wait_all(halos[1])
    stores.start(vx, vx_out)
    wait_all(got)
    stores.start(probs, probs_out)
    picks = quad_masks(F32)
    at = pl.ds(pl.multiple_of(32 * g, 32), 32)
    got = []
    for dz in (1, 3, 2, 0):
        target = mod4(spot["z"] + dz)
        b, low = lax.div(target, 2), 32 * lax.rem(target, 2)
        for n, lanes in enumerate(THIRDS):
            weigh = jnp.concatenate(
                [probs[pl.ds(pl.multiple_of(256 * (3 * b + n) + 64 * h + low, 32), 32), :] for h in range(4)], axis=0
            )
            for pair in range(2):
                made = [
                    gather_heads(
                        dot_nn(weigh, vx[2 * pair + t, pl.ds(pl.multiple_of(64 * b, 64), 128), lanes]), picks
                    )
                    for t in range(2)
                ]
                for j in range(4):
                    outgoing[4 * target + j, 16 * pair : 16 * pair + 16, lanes] = jnp.concatenate(
                        [m[8 * j : 8 * j + 8] for m in made], axis=0
                    ).astype(BF)
        for dx in range(4):
            if 4 * dz + dx > 0:
                device, index = slab_peer(spot, 4 * dz + dx)
                got.append(copies.start(outgoing.at[index], mixed.at[at], device))
    stores.start(outgoing.at[g], mixed.at[at])
    wait_all(got)
    copies.finish()
    stores.finish()


def vmem_spec():
    return pl.BlockSpec(memory_space=pltpu.VMEM)


def any_spec():
    return pl.BlockSpec(memory_space=pl.ANY)


def row_forward(x, aux, wq, wk, wv, row_gain, row_shift, scale):
    sds = jax.ShapeDtypeStruct
    n_copies = 15 * 5 + 4
    shapes = [
        ((TOKENS, LANES), BF), ((TOKENS, LANES), BF), ((4, REACH, LANES), BF), ((4, REACH, LANES), BF), ((1536, SLAB), BF),
    ]
    return pl.pallas_call(
        functools.partial(row_forward_kernel, scale),
        out_shape=(
            sds((TOKENS, LANES), BF), *[sds(*shape) for shape in shapes], sds((96, SLAB), F32), sds((TOKENS, SLAB), F32),
        ),
        in_specs=[any_spec()] * 5 + [vmem_spec()] * 2,
        out_specs=(any_spec(),) * 6 + (vmem_spec(), any_spec()),
        scratch_shapes=[
            pltpu.VMEM((GROUP, 32, LANES), BF),
            pltpu.VMEM((GROUP, 48, SLAB), BF),
            pltpu.VMEM((3, LANES, LANES), BF),
            pltpu.VMEM((TOKENS, LANES), BF),
            pltpu.VMEM((SLAB, SLAB), F32),
            pltpu.VMEM((SLAB, SLAB), F32),
            pltpu.VMEM((1536, SLAB), F32),
            pltpu.VMEM((GROUP, 96, SLAB), F32),
            pltpu.VMEM((GROUP, 32, LANES), BF),
            *[pltpu.VMEM(*shape) for shape in shapes],
            pltpu.VMEM((TOKENS, SLAB), F32),
            pltpu.VMEM((8, LANES), F32),
            pltpu.SemaphoreType.DMA((n_copies,)),
            pltpu.SemaphoreType.DMA((n_copies,)),
            pltpu.SemaphoreType.DMA((5,)),
            pltpu.SemaphoreType.DMA((8,)),
        ],
        compiler_params=pltpu.CompilerParams(collective_id=1, has_side_effects=True, vmem_limit_bytes=60 * 2**20),
    )(x, aux, wq, wk, wv, row_gain, row_shift)


def row_backward_kernel(
    scale, dm, xrow_in, q_in, kx_in, vx_in, probs_in, gaps_in, wq_in, wk_in, wv_in, squares, *rest
):
    own, row_gain, row_shift, vectors, up_bias, back, sum_col, sum_row, small_out, *rest = rest
    (
        din, dmr, act_t, partial_p, arrived, grads_s, own_k, own_v, edge_out, edge_in, gq, gk, gv, grad_act, outgoing,
        weights, small, halves, slots, vecs, xrow, q, kx, vx, probs, gaps, row_weights,
        col_total, send_sem, recv_sem, local_sem, store_sem, *groups,
    ) = rest
    spot = place()
    g = slab_place(spot)
    copies = Copies(send_sem, recv_sem)
    stores = Stores(store_sem)
    loads = [
        pltpu.make_async_copy(src, dst, local_sem.at[n])
        for n, (src, dst) in enumerate((
            (xrow_in, xrow), (dm.at[g], din.at[g]), (vx_in, vx), (probs_in, probs), (q_in, q), (kx_in, kx), (gaps_in, gaps),
            (wq_in, row_weights.at[0]), (wk_in, row_weights.at[1]), (wv_in, row_weights.at[2]),
        ))
    ]
    for copy in loads:
        copy.start()
    vector_rows(vecs, (row_gain, row_shift))
    gain, shift = vecs.at[0:1], vecs.at[1:2]
    greet(spot, slab_reach(spot)[:15] + [shifted(spot, "y", k) for k in (1, 2, 3)] + [shifted(spot, "aln", 1)])
    got = exchange(spot, copies, lambda i: dm.at[i], lambda me, k: din.at[me])

    first = start_group(spot, copies, groups[:5], squares, col_total, None, sum_col, COL_ORDERS)
    loads[0].wait()

    def normed(k, carry):
        at = pl.ds(pl.multiple_of(128 * k, 128), 128)
        scaled, _ = centre(xrow[at, :].astype(F32))
        act_t[:, at] = jnp.transpose(scaled * gain[...] + shift[...]).astype(BF)
        return carry

    lax.fori_loop(0, 4, normed, 0)
    step_all(*first)
    loads[1].wait()
    wait_all(got)

    def regroup(k, carry):
        first = din[2 * k].astype(F32)
        second = din[2 * k + 1].astype(F32)
        for s in range(4):
            at = pl.ds(pl.multiple_of(SLAB * s + 16 * k, 16), 16)
            dmr[at, :] = jnp.concatenate([first[8 * s : 8 * s + 8], second[8 * s : 8 * s + 8]], axis=0).astype(BF)
        return carry

    lax.fori_loop(0, 8, regroup, 0)
    low_picks = quad_masks(BF)
    picks = quad_masks(F32)
    mine = pl.ds(pl.multiple_of(96 * g, 32), 96)
    loads[2].wait()

    def rows_of(s, b):
        return slice(SLAB * s + 64 * b, SLAB * s + 64 * b + 64)

    for b in range(2):
        for n in range(3):
            lanes = slice(256 * n, 256 * n + 256)
            total = None
            for s in range(4):
                term = dot_nt(spread_heads(dmr[rows_of(s, b), lanes], low_picks), vx[s, 64 * b : 64 * b + 128, lanes])
                total = term if total is None else total + term
            partial_p[256 * (3 * b + n) : 256 * (3 * b + n) + 256, :] = total.astype(BF)
    got = exchange(spot, copies, lambda i: partial_p.at[pl.ds(pl.multiple_of(96 * i, 32), 96)], lambda me, k: arrived.at[k])
    step_all(*first)
    loads[3].wait()
    up, down = shifted(spot, "y", 1), shifted(spot, "y", -1)

    def scatter(weigh, source, target, which, factor):
        for n in range(3):
            lanes = slice(256 * n, 256 * n + 256)
            turned = [
                jnp.transpose(weigh[256 * (3 * b + n) : 256 * (3 * b + n) + 256, :].astype(F32)).astype(BF) for b in range(2)
            ]
            for s in range(4):
                first, second = [
                    dot_nn(turned[b], spread_heads(source[rows_of(s, b), lanes], low_picks)) * factor for b in range(2)
                ]
                edge_out[which, 0, s, :, lanes] = first[0:32].astype(BF)
                target[s, 0:32, lanes] = first[32:64]
                target[s, 32:96, lanes] = first[64:128] + second[0:64]
                target[s, 96:128, lanes] = second[64:96]
                edge_out[which, 1, s, :, lanes] = second[96:128].astype(BF)
        return [
            copies.start(edge_out.at[which, 0], edge_in.at[which, 0], down),
            copies.start(edge_out.at[which, 1], edge_in.at[which, 1], up),
        ]

    edges_v = scatter(probs, dmr, own_v, 0, 1.0)
    step_all(*first)
    wait_all(got)
    total = partial_p[mine, :].astype(F32)
    for k in range(1, GROUP):
        total = total + arrived[k].astype(F32)
    share = own[...]
    grads_s[mine, :] = (share * (total - jnp.sum(share * total, axis=-1, keepdims=True))).astype(BF)
    got = exchange(spot, copies, lambda i: grads_s.at[mine], lambda me, k: grads_s.at[mine])

    def collect(edges, which, source, target):
        wait_all(edges)
        for s in range(4):
            own_rows = source[s]
            first = own_rows[0:32] + edge_in[which, 1, s].astype(F32)
            last = own_rows[96:128] + edge_in[which, 0, s].astype(F32)
            joined = jnp.concatenate([first, own_rows[32:96], last], axis=0)
            if which == 1:
                weigh = gaps[SLAB * s : SLAB * s + SLAB, :]
                joined = joined * jnp.concatenate([weigh] * 6, axis=1)
            target[SLAB * s : SLAB * s + SLAB, :] = joined.astype(BF)

    def weight_grad(n, grad):
        for lanes in THIRDS:
            for at in THIRDS:
                weights[n, at, lanes] = dot_nn(act_t[at, :], grad[:, lanes]).astype(BF)

    collect(edges_v, 0, own_v, gv)
    weight_grad(2, gv)
    for copy in loads[4:7]:
        copy.wait()
    step_all(*first)
    wait_all(got)
    edges_k = scatter(grads_s, q, own_k, 1, scale)
    step_all(*first)
    for b in range(2):
        for n, lanes in enumerate(THIRDS):
            weigh = grads_s[256 * (3 * b + n) : 256 * (3 * b + n) + 256, :]
            for s in range(4):
                made = gather_heads(dot_nn(weigh, kx[s, 64 * b : 64 * b + 128, lanes]), picks) * scale
                gq[rows_of(s, b), lanes] = (made * wide(gaps[rows_of(s, b), :])).astype(BF)
    weight_grad(0, gq)
    collect(edges_k, 1, own_k, gk)
    weight_grad(1, gk)
    last = start_group(spot, copies, groups[5:], weights, weights, spot["aln"] * HALF, sum_row, ROW_ORDERS)
    step_all(*first)
    for copy in loads[7:10]:
        copy.wait()
    wq, wk, wv = [row_weights.at[n] for n in range(3)]
    for at in THIRDS:
        grad_act[:, at] = (
            dot_nt(gq[...], wq[at, :]) + dot_nt(gk[...], wk[at, :]) + dot_nt(gv[...], wv[at, :])
        )
    step_all(*last)

    def norm_back(k, carry):
        grad_gain, grad_shift = carry
        made = []
        for s in range(4):
            at = pl.ds(pl.multiple_of(SLAB * s + 16 * k, 16), 16)
            scaled, inverse = centre(xrow[at, :].astype(F32))
            upstream = grad_act[at, :]
            product = upstream * scaled
            grad_gain = grad_gain + product[0:8] + product[8:16]
            grad_shift = grad_shift + upstream[0:8] + upstream[8:16]
            inner = upstream * gain[...]
            middle = inner - jnp.mean(inner, axis=-1, keepdims=True)
            middle = middle - scaled * jnp.mean(inner * scaled, axis=-1, keepdims=True)
            made.append(inverse * middle)
        for pair in range(2):
            for t in range(2):
                outgoing[2 * k + t, 16 * pair : 16 * pair + 16, :] = jnp.concatenate(
                    [m[8 * t : 8 * t + 8] for m in made[2 * pair : 2 * pair + 2]], axis=0
                ).astype(BF)
        return grad_gain, grad_shift

    zero = jnp.zeros((8, LANES), F32)
    grad_gain, grad_shift = lax.fori_loop(0, 8, norm_back, (zero, zero))
    at = pl.ds(pl.multiple_of(32 * g, 32), 32)
    got = exchange(spot, copies, lambda i: outgoing.at[i], lambda me, k: back.at[at])
    stores.start(outgoing.at[g], back.at[at])
    bias_rows = [
        jnp.concatenate([up_bias[:, HALF * j : HALF * j + HALF], up_bias[:, HALF * (j + 4) : HALF * (j + 5)]], axis=1)
        for j in range(4)
    ]
    sums_here = [jnp.sum(v, axis=0, keepdims=True) for v in (grad_gain, grad_shift)]
    small[...] = jnp.concatenate(
        sums_here + [vectors[0:5, :]] + bias_rows + [jnp.zeros((5, LANES), F32)], axis=0
    )
    finish_all(*last, *first, Run(sum_small(spot, copies, small, halves, slots)))
    wait_all(got)
    copies.finish()
    stores.finish()
    small_out[...] = halves[3]


COL_ORDERS = (("y", "z", "x"), ("y", "x", "z"), ("z", "y", "x"))
ROW_ORDERS = (("x", "y", "z"), ("y", "z", "x"), ("z", "x", "y"))


def rows_of_half(which):
    return pl.ds(pl.multiple_of(which * HALF, HALF), HALF)


def row_backward(dm, kept, wq, wk, wv, squares, own, row_gain, row_shift, vectors, up_bias, scale):
    sds = jax.ShapeDtypeStruct
    n_copies = 15 * 4 + 4 + 2 * GROUP_COPIES + SMALL_COPIES
    low = pltpu.VMEM((TOKENS, LANES), BF)
    reach = pltpu.VMEM((4, REACH, LANES), BF)
    return pl.pallas_call(
        functools.partial(row_backward_kernel, scale),
        out_shape=(
            sds((TOKENS, LANES), BF), sds((5, HALF, LANES), BF), sds((3, HALF, LANES), BF), sds((16, HALF), F32),
        ),
        in_specs=[any_spec()] * 11 + [vmem_spec()] * 5,
        out_specs=(any_spec(),) * 3 + (vmem_spec(),),
        scratch_shapes=[
            pltpu.VMEM((GROUP, 32, LANES), BF),
            low,
            pltpu.VMEM((LANES, TOKENS), BF),
            pltpu.VMEM((1536, SLAB), BF),
            pltpu.VMEM((GROUP, 96, SLAB), BF),
            pltpu.VMEM((1536, SLAB), BF),
            pltpu.VMEM((4, SLAB, LANES), F32),
            pltpu.VMEM((4, SLAB, LANES), F32),
            pltpu.VMEM((2, 2, 4, 32, LANES), BF),
            pltpu.VMEM((2, 2, 4, 32, LANES), BF),
            low,
            low,
            low,
            pltpu.VMEM((TOKENS, LANES), F32),
            pltpu.VMEM((GROUP, 32, LANES), BF),
            pltpu.VMEM((3, LANES, LANES), BF),
            pltpu.VMEM((16, LANES), F32),
            pltpu.VMEM((4, 16, HALF), F32),
            pltpu.VMEM((13, 16, HALF), F32),
            pltpu.VMEM((8, LANES), F32),
            low,
            low,
            reach,
            reach,
            pltpu.VMEM((1536, SLAB), BF),
            pltpu.VMEM((TOKENS, SLAB), F32),
            pltpu.VMEM((3, LANES, LANES), BF),
            pltpu.VMEM((5, HALF, LANES), BF),
            pltpu.SemaphoreType.DMA((n_copies,)),
            pltpu.SemaphoreType.DMA((n_copies,)),
            pltpu.SemaphoreType.DMA((10,)),
            pltpu.SemaphoreType.DMA((1,)),
            *group_scratch(5),
            *group_scratch(3),
        ],
        compiler_params=pltpu.CompilerParams(collective_id=2, has_side_effects=True, vmem_limit_bytes=60 * 2**20),
    )(dm, *kept, wq, wk, wv, squares, own, row_gain, row_shift, vectors, up_bias)


TOKENS = 512
TILE = 256
THIRDS = [slice(256 * n, 256 * n + 256) for n in range(3)]


def to_columns():
    row = lax.broadcasted_iota(jnp.int32, (TOKENS, TOKENS), 0)
    token = lax.broadcasted_iota(jnp.int32, (TOKENS, TOKENS), 1)
    want = lax.rem(row, 64) * 8 + lax.div(row, 64)
    return (token == want).astype(F32).astype(BF)


def to_sequences():
    row = lax.broadcasted_iota(jnp.int32, (TOKENS, TOKENS), 0)
    token = lax.broadcasted_iota(jnp.int32, (TOKENS, TOKENS), 1)
    want = lax.rem(row, 8) * 64 + lax.div(row, 8)
    return (token == want).astype(F32).astype(BF)


def rows_loop(count, body, init=0):
    def step(k, carry):
        return body(pl.ds(pl.multiple_of(64 * k, 64), 64), carry)

    return lax.fori_loop(0, count // 64, step, init)


def normed_rows(values, gain, shift, act, act_t):
    def body(k, carry):
        at = pl.ds(pl.multiple_of(128 * k, 128), 128)
        scaled, _ = centre(values[at, :])
        made = scaled * gain[...] + shift[...]
        act[at, :] = made.astype(BF)
        if act_t is not None:
            act_t[:, at] = jnp.transpose(made).astype(BF)
        return carry

    lax.fori_loop(0, TOKENS // 128, body, 0)


def norm_back_rows(values, upstream, gain, residual, out):
    def body(at, carry):
        grad_gain, grad_shift = carry
        scaled, inverse = centre(values[at, :])
        up = upstream[at, :]
        product = up * scaled
        for r in range(8):
            grad_gain = grad_gain + product[8 * r : 8 * r + 8]
            grad_shift = grad_shift + up[8 * r : 8 * r + 8]
        inner = up * gain[...]
        middle = inner - jnp.mean(inner, axis=-1, keepdims=True)
        middle = middle - scaled * jnp.mean(inner * scaled, axis=-1, keepdims=True)
        out[at, :] = residual[at, :].astype(F32) + inverse * middle
        return grad_gain, grad_shift

    zero = jnp.zeros((8, LANES), F32)
    return rows_loop(TOKENS, body, (zero, zero))


def column_probs(scale, queries, keys, at, lanes, picks):
    heads = spread_heads(queries[at, lanes], picks)
    scores = dot_nt(keys[at, lanes], heads) * scale
    expo = jnp.exp(scores - jnp.max(scores, axis=0, keepdims=True))
    return heads, expo / jnp.sum(expo, axis=0, keepdims=True)


def column_kernel(
    scale, x, mixed, cot, wq, wk, wv, col_out, row_out, up, down,
    col_gain, col_shift, mlp_gain, mlp_shift, down_bias_in, up_bias_in,
    result_out, grad_inputs_out, grad_row_mixed_out, squares_out, sum_mlp, vectors, grad_up_bias,
    squares, vecs, up_bias, weights, up_tiles, down_tiles, raw, order, mixed_cs, act, act_t, after_row, after_col, made, grad_act,
    queries, keys, values, col_mixed, cot_cs, keep, give, load_sem, tile_sem, out_sem, send_sem, recv_sem, *groups,
):
    spot = place()
    side = spot["aln"]
    copies = Copies(send_sem, recv_sem)
    stores = Stores(out_sem)
    vector_rows(vecs, (col_gain, col_shift, mlp_gain, mlp_shift, down_bias_in))
    up_bias[...] = up_bias_in[...].reshape(1, 4 * LANES)
    loads = [
        pltpu.make_async_copy(src, dst, load_sem.at[n])
        for n, (src, dst) in enumerate((
            (mixed, raw.at[1]), (x, raw.at[0]), (row_out, weights.at[4]), (wq, weights.at[0]), (wk, weights.at[1]),
            (wv, weights.at[2]), (col_out, weights.at[3]), (cot, raw.at[2]),
        ))
    ]
    for copy in loads:
        copy.start()
    steps = 2 * 2 * 3

    def spot_of(j):
        half = side if (j // 3) % 2 == 0 else 1 - side
        return half, pl.multiple_of(half * (4 * HALF) + (j // 6) * LANES + (j % 3) * TILE, TILE)

    def fetch(j):
        _, at = spot_of(j)
        slot = j % 3
        return [
            pltpu.make_async_copy(up.at[:, pl.ds(at, TILE)], up_tiles.at[slot], tile_sem.at[slot, 0]),
            pltpu.make_async_copy(down.at[pl.ds(at, TILE)], down_tiles.at[slot], tile_sem.at[slot, 1]),
        ]

    greet(spot, torus_reach(spot))
    order[...] = to_columns()
    loads[0].wait()
    for lanes in THIRDS:
        mixed_cs[:, lanes] = dot_nn(order[...], raw[1, :, lanes]).astype(BF)
    loads[1].wait()
    loads[2].wait()
    for lanes in THIRDS:
        after_row[:, lanes] = dot_nn(order[...], raw[0, :, lanes]) + dot_nn(mixed_cs[...], weights[4, :, lanes])
    normed_rows(after_row, vecs.at[0:1], vecs.at[1:2], act, None)
    for j in range(2):
        for copy in fetch(j):
            copy.start()
    for n, out in enumerate((queries, keys, values)):
        loads[3 + n].wait()
        for lanes in THIRDS:
            out[:, lanes] = dot_nn(act[...], weights[n, :, lanes]).astype(BF)
    low_picks, picks = quad_masks(BF), quad_masks(F32)

    def attend(k, carry):
        for at, lanes in [
            (pl.ds(pl.multiple_of(256 * k + 64 * c, 64), 64), lanes) for c in range(4) for lanes in THIRDS
        ]:
            _, probs = column_probs(scale, queries, keys, at, lanes, low_picks)
            mixes = dot_tn(probs.astype(BF), values[at, lanes])
            col_mixed[at, lanes] = gather_heads(mixes, picks).astype(BF)
        return carry

    lax.fori_loop(0, 2, attend, 0)
    loads[6].wait()
    for lanes in THIRDS:
        after_col[:, lanes] = after_row[:, lanes] + dot_nn(col_mixed[...], weights[3, :, lanes])
    gain, shift, down_bias = vecs.at[2:3], vecs.at[3:4], vecs.at[4:5]
    normed_rows(after_col, gain, shift, act, act_t)
    loads[7].wait()
    for lanes in THIRDS:
        cot_cs[:, lanes] = dot_nn(order[...], raw[2, :, lanes]).astype(BF)
    order[...] = to_sequences()

    def mlp_group(i):
        return start_group(
            spot, copies, groups[5 * i : 5 * i + 5], (keep.at[i], give.at[i]), keep.at[i], 0, sum_mlp.at[i], MLP_ORDERS[i])

    for j in range(steps):
        half, at = spot_of(j)
        slot, i = j % 3, j // 6
        if j + 2 < steps:
            for copy in fetch(j + 2):
                copy.start()
        for copy in fetch(j):
            copy.wait()
        hidden_pre = dot_nn(act[...], up_tiles[slot]) + up_bias[:, pl.ds(at, TILE)]
        grad_hidden = dot_nt(cot_cs[...], down_tiles[slot])
        phi = 0.5 + 0.5 * lax.erf(hidden_pre * (1.0 / math.sqrt(2.0)))
        slope = phi + hidden_pre * jnp.exp(-0.5 * hidden_pre * hidden_pre) * (1.0 / math.sqrt(2.0 * math.pi))
        hidden = (hidden_pre * phi).astype(BF)
        pre = (grad_hidden * slope).astype(BF)
        tall = keep if (j // 3) % 2 == 0 else give
        hidden_t = jnp.transpose(hidden)
        lanes_here = slice(TILE * (j % 3), TILE * (j % 3) + TILE)
        for lanes in THIRDS:
            if j == 0:
                made[:, lanes] = dot_nn(hidden, down_tiles[slot, :, lanes])
                grad_act[:, lanes] = dot_nt(pre, up_tiles[slot, lanes, :])
            else:
                made[:, lanes] += dot_nn(hidden, down_tiles[slot, :, lanes])
                grad_act[:, lanes] += dot_nt(pre, up_tiles[slot, lanes, :])
            grad = dot_nn(hidden_t, cot_cs[:, lanes]).astype(BF)
            for part in range(2):
                low, high = max(TILE * (j % 3), HALF * part), min(TILE * (j % 3) + TILE, HALF * part + HALF)
                if low < high:
                    tall[i, part, low - HALF * part : high - HALF * part, lanes] = (
                        grad[low - TILE * (j % 3) : high - TILE * (j % 3)]
                    )
        for which, out in ((side, keep), (1 - side, give)):
            out[i, 2 + half, :, lanes_here] = dot_nn(act_t[rows_of_half(which), :], pre).astype(BF)
        grad_up_bias[:, pl.ds(at, TILE)] = jnp.sum(pre.astype(F32), axis=0, keepdims=True)
        if j in (7, 9, 11):
            step_all(*first)
        if j == 5:
            first = mlp_group(0)
        if j == 11:
            second = mlp_group(1)
    for lanes in THIRDS:
        full = after_col[:, lanes] + (made[:, lanes] + down_bias[:, lanes])
        raw[2, :, lanes] = dot_nn(order[...], full.astype(BF)).astype(BF)
    stores.start(raw.at[2], result_out)
    sum_gain, sum_shift = norm_back_rows(after_col, grad_act, gain, cot_cs, after_col)

    def bias_sum(at, carry):
        values_here = cot_cs[at, :].astype(F32)
        for r in range(8):
            carry = carry + values_here[8 * r : 8 * r + 8]
        return carry

    bias = rows_loop(TOKENS, bias_sum, jnp.zeros((8, LANES), F32))
    branch, grad_mixed = raw.at[0], raw.at[1]

    def rounded(at, carry):
        branch[at, :] = after_col[at, :].astype(BF)
        return carry

    rows_loop(TOKENS, rounded)
    step_all(*first, *second)
    for lanes in THIRDS:
        grad_mixed[:, lanes] = dot_nt(branch[...], weights[3, lanes, :]).astype(BF)
    gain, shift = vecs.at[0:1], vecs.at[1:2]
    normed_rows(after_row, gain, shift, act, act_t)

    def attend_back(k, carry):
        for at, lanes in [
            (pl.ds(pl.multiple_of(128 * k + 64 * c, 64), 64), lanes) for c in range(2) for lanes in THIRDS
        ]:
            heads, probs = column_probs(scale, queries, keys, at, lanes, low_picks)
            upstream = spread_heads(grad_mixed[at, lanes], low_picks)
            grad_probs = dot_nt(values[at, lanes], upstream)
            grad_scores = probs * (grad_probs - jnp.sum(probs * grad_probs, axis=0, keepdims=True))
            grad_scores = grad_scores.astype(BF)
            gq = (gather_heads(dot_tn(grad_scores, keys[at, lanes]), picks) * scale).astype(BF)
            gk = (dot_nn(grad_scores, heads) * scale).astype(BF)
            gv = dot_nn(probs.astype(BF), upstream).astype(BF)
            queries[at, lanes] = gq
            keys[at, lanes] = gk
            values[at, lanes] = gv
        return carry

    for n, runs in enumerate(((*first, *second), (), (*first, *second), second)):
        lax.fori_loop(n, n + 1, attend_back, 0)
        step_all(*runs)
    for lanes in THIRDS:
        grad_act[:, lanes] = (
            dot_nt(queries[...], weights[0, lanes, :])
            + dot_nt(keys[...], weights[1, lanes, :])
            + dot_nt(values[...], weights[2, lanes, :])
        )
    for at in THIRDS:
        squares[0, at, :] = dot_tn(col_mixed[:, at], branch[...]).astype(BF)
    stores.start(squares.at[0], squares_out.at[0])
    step_all(*first, *second)
    grad_gain, grad_shift = norm_back_rows(after_row, grad_act, gain, after_col, after_row)
    sums = [jnp.sum(v, axis=0, keepdims=True) for v in (grad_gain, grad_shift, sum_gain, sum_shift, bias)]
    vectors[...] = jnp.concatenate(sums + [jnp.zeros((3, LANES), F32)], axis=0)

    def rounded_row(at, carry):
        values_here = after_row[at, :]
        high = values_here.astype(BF)
        branch[at, :] = high
        act[at, :] = (values_here - high.astype(F32)).astype(BF)
        return carry

    rows_loop(TOKENS, rounded_row)
    for lanes in THIRDS:
        grad_mixed[:, lanes] = dot_nt(branch[...], weights[4, lanes, :]).astype(BF)
    for lanes in THIRDS:
        cot_cs[:, lanes] = dot_nn(order[...], grad_mixed[:, lanes]).astype(BF)
        made[:, lanes] = dot_nn(order[...], branch[:, lanes]) + dot_nn(order[...], act[:, lanes])
    stores.start(cot_cs, grad_row_mixed_out)
    stores.start(made, grad_inputs_out)
    step_all(*first, *second)
    for n, grad in enumerate((queries, keys, values)):
        for at in THIRDS:
            squares[1 + n, at, :] = dot_nn(act_t[at, :], grad[...]).astype(BF)
        stores.start(squares.at[1 + n], squares_out.at[1 + n])
    for at in THIRDS:
        squares[4, at, :] = dot_tn(mixed_cs[:, at], branch[...]).astype(BF)
    stores.start(squares.at[4], squares_out.at[4])
    finish_all(*first, *second)
    copies.finish()
    stores.finish()


MLP_ORDERS = (
    (("x", "y", "z"), ("y", "z", "x"), ("z", "x", "y")),
    (("x", "z", "y"), ("y", "x", "z"), ("z", "y", "x")),
)


def column_part(
    x, mixed, cot, wq, wk, wv, col_out, row_out, up, down, col_gain, col_shift, mlp_gain, mlp_shift, down_bias, up_bias, scale
):
    sds = jax.ShapeDtypeStruct
    hidden = up.shape[1]
    tokens = sds((TOKENS, LANES), BF)
    low = pltpu.VMEM((TOKENS, LANES), BF)
    full = pltpu.VMEM((TOKENS, LANES), F32)
    n_copies = 2 * GROUP_COPIES
    return pl.pallas_call(
        functools.partial(column_kernel, scale),
        out_shape=(
            tokens, sds((TOKENS, LANES), F32), tokens, sds((5, LANES, LANES), BF), sds((2, 4, HALF, LANES), BF),
            sds((8, LANES), F32), sds((1, hidden), F32),
        ),
        in_specs=[any_spec()] * 10 + [vmem_spec()] * 6,
        out_specs=(any_spec(),) * 5 + (vmem_spec(),) * 2,
        scratch_shapes=[
            pltpu.VMEM((5, LANES, LANES), BF),
            pltpu.VMEM((8, LANES), F32),
            pltpu.VMEM((1, hidden), F32),
            pltpu.VMEM((5, LANES, LANES), BF),
            pltpu.VMEM((3, LANES, TILE), BF),
            pltpu.VMEM((3, TILE, LANES), BF),
            pltpu.VMEM((3, TOKENS, LANES), BF),
            pltpu.VMEM((TOKENS, TOKENS), BF),
            low, low, pltpu.VMEM((LANES, TOKENS), BF), full, full, full, full, low, low, low, low, low,
            pltpu.VMEM((2, 4, HALF, LANES), BF),
            pltpu.VMEM((2, 4, HALF, LANES), BF),
            pltpu.SemaphoreType.DMA((8,)),
            pltpu.SemaphoreType.DMA((3, 2)),
            pltpu.SemaphoreType.DMA((8,)),
            pltpu.SemaphoreType.DMA((n_copies,)),
            pltpu.SemaphoreType.DMA((n_copies,)),
            *group_scratch(4),
            *group_scratch(4),
        ],
        compiler_params=pltpu.CompilerParams(collective_id=3, has_side_effects=True, vmem_limit_bytes=60 * 2**20),
    )(
        x, mixed, cot, wq, wk, wv, col_out, row_out, up, down,
        col_gain, col_shift, mlp_gain, mlp_shift, down_bias, up_bias,
    )


def finish_kernel(base, back, mlp, col, row, small, total, up, down, *rest):
    squares, vectors, bias = rest[:8], rest[8:15], rest[15]
    total[...] = base[...] + back[...].astype(F32)
    for i in range(2):
        for n in range(2):
            down[2 * i + n] = mlp[i, n].astype(F32)
            k = 2 * n + i
            up[:, LANES * k : LANES * k + LANES] = mlp[i, 2 + n].astype(F32)
    for n in range(5):
        squares[n][...] = col[n].astype(F32)
    for n in range(3):
        squares[5 + n][...] = row[n].astype(F32)
    for n in range(7):
        vectors[n][...] = small[n, :]
    for n in range(4):
        bias[HALF * n : HALF * n + HALF] = small[7 + n, :]


def finish(base, back, mlp, col, row, small):
    steps = 8
    rows = HALF // steps
    sds = jax.ShapeDtypeStruct
    tokens = pl.BlockSpec((TOKENS // steps, LANES), lambda i: (i, 0))
    square = pl.BlockSpec((rows, LANES), lambda i: (i, 0))
    return pl.pallas_call(
        finish_kernel,
        grid=(steps,),
        out_shape=[
            sds((TOKENS, LANES), F32), sds((HALF, 4 * LANES), F32), sds((4, HALF, LANES), F32),
            *[sds((HALF, LANES), F32)] * 8, *[sds((HALF,), F32)] * 7, sds((4 * HALF,), F32),
        ],
        in_specs=[
            tokens, tokens,
            pl.BlockSpec((2, 4, rows, LANES), lambda i: (0, 0, i, 0)),
            pl.BlockSpec((5, rows, LANES), lambda i: (0, i, 0)),
            pl.BlockSpec((3, rows, LANES), lambda i: (0, i, 0)),
            pl.BlockSpec((16, HALF), lambda i: (0, 0)),
        ],
        out_specs=[
            tokens,
            pl.BlockSpec((rows, 4 * LANES), lambda i: (i, 0)),
            pl.BlockSpec((4, rows, LANES), lambda i: (0, i, 0)),
            *[square] * 8, *[pl.BlockSpec((HALF,), lambda i: (0,))] * 7, pl.BlockSpec((4 * HALF,), lambda i: (0,)),
        ],
        compiler_params=pltpu.CompilerParams(vmem_limit_bytes=60 * 2**20),
    )(base, back, mlp, col, row, small)


def side_inputs(gap_flags, band_mask):
    col = lax.axis_index("col")
    weights = (1.0 - GAP_DROP * gap_flags.astype(F32)).reshape(GROUP, 32, 1)
    query = 8 * lax.rem(col, 8) + jnp.arange(8, dtype=jnp.int32)[:, None]
    key = jnp.arange(SLAB, dtype=jnp.int32)[None, :]
    offset = key - query
    chosen = (offset[:, :, None] == jnp.arange(2 * BAND + 1, dtype=jnp.int32)) & (band_mask[:, None, :] == 1)
    where = 64 * lax.div(col, 8) + key - BAND
    allowed = (jnp.any(chosen, axis=-1) | (offset == BAND)) & (where >= 0) & (where < COLS)
    allowed = jnp.broadcast_to(allowed.astype(F32)[None], (GROUP, 8, SLAB))
    weights = jnp.broadcast_to(weights, (GROUP, 32, SLAB))
    return jnp.concatenate([weights, allowed, jnp.zeros((GROUP, 8, SLAB), F32)], axis=1).astype(BF)


def per_device(
    inputs,
    gap_flags,
    band_mask,
    row_gain,
    row_shift,
    row_query,
    row_key,
    row_value,
    row_out,
    col_gain,
    col_shift,
    col_query,
    col_key,
    col_value,
    col_out,
    mlp_gain,
    mlp_shift,
    mlp_up,
    up_bias,
    mlp_down,
    down_bias,
    cotangent,
):
    seqs, width_cols, model = (inputs.shape[1], inputs.shape[2], inputs.shape[3])
    low_tokens = (seqs * width_cols, model)
    row_scale = 1.0 / math.sqrt(HD * seqs)
    col_scale = 1.0 / math.sqrt(HD)
    aux = side_inputs(gap_flags[0], band_mask[0])
    mixed_low, *kept_row, own, gaps = row_forward(
        inputs.reshape(GROUP, 32, model), aux, row_query, row_key, row_value, row_gain, row_shift, row_scale
    )
    result, grad_after_row, grad_row_mixed, squares, sum_mlp, vectors, grad_up_bias = column_part(
        inputs.reshape(low_tokens), mixed_low, cotangent.reshape(low_tokens), col_query, col_key, col_value, col_out,
        row_out, mlp_up, mlp_down, col_gain, col_shift, mlp_gain, mlp_shift, down_bias, up_bias, col_scale,
    )
    back_row, sum_col, sum_row, small_sum = row_backward(
        grad_row_mixed.reshape(GROUP, 32, model), (*kept_row, gaps), row_query, row_key, row_value, squares, own, row_gain,
        row_shift, vectors, grad_up_bias, row_scale,
    )
    grad_inputs, up_sum, down_sum, co_sum, cq_sum, ck_sum, cv_sum, ro_sum, rq_sum, rk_sum, rv_sum, *vector_sums = finish(
        grad_after_row, back_row, sum_mlp, sum_col, sum_row, small_sum
    )
    return (
        result.reshape(inputs.shape),
        grad_inputs.reshape(inputs.shape),
        vector_sums[0],
        vector_sums[1],
        rq_sum,
        rk_sum,
        rv_sum,
        ro_sum,
        vector_sums[2],
        vector_sums[3],
        cq_sum,
        ck_sum,
        cv_sum,
        co_sum,
        vector_sums[4],
        vector_sums[5],
        up_sum,
        vector_sums[7],
        down_sum.reshape(4 * HALF, model),
        vector_sums[6],
    )


def solution(mesh):
    in_specs = (
        P("aln", None, "col", None),
        P("aln", None, "col"),
        P("aln", "col", None),
        P(),
        P(),
        P(),
        P(),
        P(),
        P(),
        P(),
        P(),
        P(),
        P(),
        P(),
        P(),
        P(),
        P(),
        P(),
        P(),
        P(),
        P(),
        P("aln", None, "col", None),
    )
    out_specs = (
        P("aln", None, "col", None),
        P("aln", None, "col", None),
        P("aln"),
        P("aln"),
        P("aln", None),
        P("aln", None),
        P("aln", None),
        P("aln", None),
        P("aln"),
        P("aln"),
        P("aln", None),
        P("aln", None),
        P("aln", None),
        P("aln", None),
        P("aln"),
        P("aln"),
        P("aln", None),
        P("aln"),
        P("aln", None),
        P("aln"),
    )
    return jax.shard_map(
        per_device, mesh=mesh, in_specs=in_specs, out_specs=out_specs, check_vma=False
    )
```

```python
import functools
import math

import jax
import jax.numpy as jnp
from jax import lax
from jax.experimental import pallas as pl
from jax.experimental.pallas import tpu as pltpu
from jax.sharding import PartitionSpec as P

H = 12
HD = 64
COLS = 512
BAND = 32


GAP_DROP = 0.75
MESH = pl.DeviceIdType.MESH
LANES = 768
HALF = 384
THIRD = 128
QUARTER = 32
PIECE = 16
BF = jnp.bfloat16
F32 = jnp.float32


def place():
    col = lax.axis_index("col")
    return {
        "aln": lax.axis_index("aln"),
        "x": lax.rem(col, 4),
        "z": lax.rem(lax.div(col, 4), 4),
        "y": lax.div(col, 16),
    }


def device_at(spot):
    return (spot["aln"], spot["y"] * 16 + spot["z"] * 4 + spot["x"])


def mod4(v):
    return lax.rem(v + 4, 4)


def shifted(spot, axis, step):
    if axis == "aln":
        return device_at({**spot, "aln": 1 - spot["aln"]})
    return device_at({**spot, axis: mod4(spot[axis] + step)})


def greet(spot, reach):
    barrier = pltpu.get_barrier_semaphore()
    for peer in reach:
        pl.semaphore_signal(barrier, inc=1, device_id=peer, device_id_type=MESH)
    pl.semaphore_wait(barrier, len(reach))


def torus_reach(spot):
    return [shifted(spot, a, s) for a in "xyz" for s in (1, 2, 3)] + [shifted(spot, "aln", 1)]


def block(rows, count, lanes=0, width=LANES):
    return (slice(None), pl.ds(pl.multiple_of(rows, 16), count), pl.ds(pl.multiple_of(lanes, 128), width))


def add_into(dst, at, sources):
    total = dst[at]
    for ref, near in sources:
        total = total + ref[near]
    dst[at] = total


class Copies:
    def __init__(self, send_sem, recv_sem):
        self.send_sem, self.recv_sem, self.used, self.sent = send_sem, recv_sem, 0, []

    def start(self, src, dst, device):
        k = self.used
        self.used += 1
        copy = pltpu.make_async_remote_copy(
            src_ref=src, dst_ref=dst, send_sem=self.send_sem.at[k], recv_sem=self.recv_sem.at[k],
            device_id=device, device_id_type=MESH)
        copy.start()
        self.sent.append(copy)
        return copy

    def finish(self):
        for copy in self.sent:
            copy.wait_send()
        self.sent = []


def wait_all(started):
    for copy in started:
        copy.wait_recv()


GROUP_COPIES = 60


def reduce_third(spot, copies, load, give, total, base, swap, recv, pieces, out, row, store_sem, order):
    first, second, third = order
    if load is not None:
        load.start()
    got = copies.start(give, swap, shifted(spot, "aln", 1))
    yield
    if load is not None:
        load.wait()
    got.wait_recv()
    for r in range(4):
        add_into(total, block(base + QUARTER * r, QUARTER), [(swap, block(QUARTER * r, QUARTER))])
    m = spot[first]
    up, down = shifted(spot, first, 1), shifted(spot, first, -1)

    def chunk(k, lane):
        return block(base + mod4(k) * QUARTER, QUARTER, lane, HALF)

    def slot(j):
        return block(QUARTER * (j % 3), QUARTER, HALF * (j // 3), HALF)

    relay_up = copies.start(total.at[chunk(m + 2, 0)], recv.at[slot(0)], up)
    relay_down = copies.start(total.at[chunk(m + 2, HALF)], recv.at[slot(3)], down)
    early_up = copies.start(total.at[chunk(m + 1, HALF)], recv.at[slot(1)], up)
    early_down = copies.start(total.at[chunk(m - 1, 0)], recv.at[slot(4)], down)
    yield
    relay_up.wait_recv()
    add_into(total, chunk(m + 1, 0), [(recv, slot(0))])
    late_up = copies.start(total.at[chunk(m + 1, 0)], recv.at[slot(2)], up)
    relay_down.wait_recv()
    add_into(total, chunk(m - 1, HALF), [(recv, slot(3))])
    late_down = copies.start(total.at[chunk(m - 1, HALF)], recv.at[slot(5)], down)
    yield
    wait_all([early_up, early_down, late_up, late_down])
    add_into(total, chunk(m, 0), [(recv, slot(2)), (recv, slot(4))])
    add_into(total, chunk(m, HALF), [(recv, slot(1)), (recv, slot(5))])
    n = spot[second]

    def piece(k, start):
        return block(start + m * QUARTER + lax.div(mod4(k), 2) * PIECE, PIECE, lax.rem(mod4(k), 2) * HALF, HALF)

    got = [copies.start(total.at[piece(n + d, base)], pieces.at[d - 1], shifted(spot, second, d)) for d in (1, 3, 2)]
    yield
    wait_all(got)
    own = total[piece(n, base)].astype(F32)
    for d in range(3):
        own = own + pieces[d].astype(F32)
    spread = spot[third]
    pieces[3 + spread] = own.astype(BF)
    got = [copies.start(pieces.at[3 + spread], pieces.at[3 + spread], shifted(spot, third, d)) for d in (1, 3, 2)]
    yield
    wait_all(got)
    own = pieces[3].astype(F32)
    for d in range(1, 4):
        own = own + pieces[3 + d].astype(F32)
    total[piece(n, base)] = own.astype(BF)
    store = pltpu.make_async_copy(total.at[piece(n, base)], out.at[piece(n, row)], store_sem)
    store.start()
    got = [copies.start(total.at[piece(n, base)], out.at[piece(n, row)], shifted(spot, second, d)) for d in (1, 3, 2)]
    yield
    store.wait()
    wait_all(got)

    def whole(k, lane=0, width=LANES):
        return out.at[block(row + mod4(k) * QUARTER, QUARTER, lane, width)]

    go_up = copies.start(whole(m), whole(m), up)
    go_down = copies.start(whole(m), whole(m), down)
    yield
    go_up.wait_recv()
    on_up = copies.start(whole(m - 1, 0, HALF), whole(m - 1, 0, HALF), up)
    go_down.wait_recv()
    on_down = copies.start(whole(m + 1, HALF, HALF), whole(m + 1, HALF, HALF), down)
    yield
    wait_all([on_up, on_down])


def sum_small(spot, copies, small, halves, slots):
    mine, other = spot["aln"], 1 - spot["aln"]

    def half(which):
        return (slice(None), pl.ds(pl.multiple_of(which * HALF, HALF), HALF))

    swap = copies.start(small.at[half(other)], slots.at[12], shifted(spot, "aln", 1))
    yield
    swap.wait_recv()
    halves[0] = small[half(mine)] + slots[12]
    for n, axis in enumerate(("x", "y", "z")):
        m = spot[axis]
        slots[4 * n + m] = halves[n]
        got = [copies.start(slots.at[4 * n + m], slots.at[4 * n + m], shifted(spot, axis, k)) for k in (1, 2, 3)]
        yield
        wait_all(got)
        halves[n + 1] = (slots[4 * n] + slots[4 * n + 1]) + (slots[4 * n + 2] + slots[4 * n + 3])


SMALL_COPIES = 10


class Run:
    def __init__(self, steps):
        self.steps, self.live = steps, True

    def step(self):
        if self.live:
            self.live = next(self.steps, "end") != "end"


def step_all(*runs):
    for run in runs:
        run.step()


def finish_all(*runs):
    while any(run.live for run in runs):
        step_all(*runs)


def vector_rows(scratch, vectors):
    for n, vector in enumerate(vectors):
        scratch[n : n + 1, :] = vector[...].reshape(1, LANES)


class Stores:
    def __init__(self, sems):
        self.sems, self.copies = sems, []

    def start(self, src, dst):
        copy = pltpu.make_async_copy(src, dst, self.sems.at[len(self.copies)])
        copy.start()
        self.copies.append(copy)
        return copy

    def finish(self):
        for copy in self.copies:
            copy.wait()


def group_scratch(n):
    return [
        pltpu.VMEM((n, HALF, LANES), BF),
        pltpu.VMEM((3, n, 3 * QUARTER, LANES), BF),
        pltpu.VMEM((3, 7, n, PIECE, HALF), BF),
        pltpu.SemaphoreType.DMA((3,)),
        pltpu.SemaphoreType.DMA((3,)),
    ]


def start_group(spot, copies, scratch, source, total, base, out, orders):
    swap, recv, pieces, load_sem, store_sem = scratch
    other, side = 1 - spot["aln"], spot["aln"]
    runs = []
    for t in range(3):
        rows = slice(THIRD * t, THIRD * t + THIRD)
        if isinstance(source, tuple):
            give, load, start = source[1].at[:, rows], None, THIRD * t
        else:
            give = source.at[:, pl.ds(pl.multiple_of(other * HALF + THIRD * t, THIRD), THIRD)]
            if base is None:
                keep = source.at[:, pl.ds(pl.multiple_of(side * HALF + THIRD * t, THIRD), THIRD)]
                load, start = pltpu.make_async_copy(keep, total.at[:, rows], load_sem.at[t]), THIRD * t
            else:
                load, start = None, base + THIRD * t
        runs.append(Run(reduce_third(
            spot, copies, load, give, total, start, swap.at[:, rows], recv.at[t], pieces.at[t], out, THIRD * t,
            store_sem.at[t], orders[t])))
    step_all(*runs)
    return runs


GROUP = 16
SLAB = 128
REACH = 192
EPSILON = 1e-05
NEG_FILL = -1000000000.0


def dot_nn(a, b):
    return lax.dot_general(a, b, (((1,), (0,)), ((), ())), preferred_element_type=F32)


def dot_nt(a, b):
    return lax.dot_general(a, b, (((1,), (1,)), ((), ())), preferred_element_type=F32)


def dot_tn(a, b):
    return lax.dot_general(a, b, (((0,), (0,)), ((), ())), preferred_element_type=F32)


def quad_masks(dtype):
    lane = lax.broadcasted_iota(jnp.int32, (1, 256), 1)
    return [((lane >= 64 * h) & (lane < 64 * h + 64)).astype(F32).astype(dtype) for h in range(4)]


def spread_heads(block, masks):
    return jnp.concatenate([block * m for m in masks], axis=0)


def gather_heads(block, masks):
    n = block.shape[0] // 4
    out = block[0:n] * masks[0]
    for h in range(1, 4):
        out = out + block[n * h : n * h + n] * masks[h]
    return out


SLAB_ORDER = (1, 4, 3, 12, 2, 8, 5, 7, 13, 15, 6, 9, 11, 14, 10)


def slab_place(spot):
    return spot["z"] * 4 + spot["x"]


def slab_peer(spot, k):
    dz, dx = k // 4, k % 4
    there = {**spot, "z": mod4(spot["z"] + dz), "x": mod4(spot["x"] + dx)}
    return device_at(there), slab_place(there)


def exchange(spot, copies, src_of, dst_of):
    out = []
    for k in SLAB_ORDER:
        device, index = slab_peer(spot, k)
        out.append(copies.start(src_of(index), dst_of(slab_place(spot), k), device))
    return out


def slab_reach(spot):
    return [slab_peer(spot, k)[0] for k in range(1, GROUP)] + [shifted(spot, "y", 1), shifted(spot, "y", -1)]


def centre(rows):
    center = rows - jnp.mean(rows, axis=-1, keepdims=True)
    inverse = lax.rsqrt(jnp.mean(center * center, axis=-1, keepdims=True) + EPSILON)
    return center * inverse, inverse


def wide(weights):
    return jnp.concatenate([weights, weights], axis=1)


def row_forward_kernel(
    scale, x, aux, wq, wk, wv, row_gain, row_shift,
    mixed, xrow_out, q_out, kx_out, vx_out, probs_out, own, gaps_out,
    xin, auxin, weights, act, masks_in, mask_pick, scores, arrived, outgoing, xrow, q, kx, vx, probs, gaps, vecs,
    send_sem, recv_sem, local_sem, store_sem,
):
    spot = place()
    g = slab_place(spot)
    copies = Copies(send_sem, recv_sem)
    stores = Stores(store_sem)
    locals_ = [
        pltpu.make_async_copy(aux.at[g], auxin.at[g], local_sem.at[0]),
        pltpu.make_async_copy(x.at[g], xin.at[g], local_sem.at[1]),
        pltpu.make_async_copy(wk, weights.at[0], local_sem.at[2]),
        pltpu.make_async_copy(wv, weights.at[1], local_sem.at[3]),
        pltpu.make_async_copy(wq, weights.at[2], local_sem.at[4]),
    ]
    for copy in locals_:
        copy.start()
    vector_rows(vecs, (row_gain, row_shift))
    gain, shift = vecs.at[0:1], vecs.at[1:2]
    greet(spot, slab_reach(spot))
    got = exchange(spot, copies, lambda i: x.at[i], lambda me, k: xin.at[me])
    got_aux = exchange(spot, copies, lambda i: aux.at[i], lambda me, k: auxin.at[me])
    locals_[0].wait()
    locals_[1].wait()

    def regroup_row(row):
        def body(h, carry):
            k = 2 * row + h
            first = xin[2 * k].astype(F32)
            second = xin[2 * k + 1].astype(F32)
            side = auxin[2 * k].astype(F32)
            other = auxin[2 * k + 1].astype(F32)
            for s in range(4):
                rows = jnp.concatenate([first[8 * s : 8 * s + 8], second[8 * s : 8 * s + 8]], axis=0)
                at = pl.ds(pl.multiple_of(SLAB * s + 16 * k, 16), 16)
                xrow[at, :] = rows.astype(BF)
                scaled, _ = centre(rows)
                act[at, :] = (scaled * gain[...] + shift[...]).astype(BF)
                gaps[at, :] = jnp.concatenate([side[8 * s : 8 * s + 8], other[8 * s : 8 * s + 8]], axis=0)
            at = pl.ds(pl.multiple_of(16 * k, 16), 16)
            masks_in[at, :] = jnp.concatenate([side[32:40], other[32:40]], axis=0)
            return carry

        lax.fori_loop(0, 2, body, 0)

    by_step = dict(zip(SLAB_ORDER, zip(got, got_aux)))
    for dz in (0, 3, 1, 2):
        for dx in range(4):
            if 4 * dz + dx > 0:
                wait_all(by_step[4 * dz + dx])
        regroup_row(mod4(spot["z"] - dz))
    stores.start(xrow, xrow_out)
    stores.start(gaps, gaps_out)
    halos = [[], []]
    up, down = shifted(spot, "y", 1), shifted(spot, "y", -1)

    def project(which):
        target = (kx, vx)[which]
        locals_[2 + which].wait()
        for lanes in THIRDS:
            made = dot_nn(act[...], weights[which, :, lanes])
            if which == 0:
                made = made * wide(gaps[...])
            for s in range(4):
                target[s, 32:160, lanes] = made[SLAB * s : SLAB * s + SLAB].astype(BF)
            halos[which] += [
                copies.start(target.at[:, 128:160, lanes], target.at[:, 0:32, lanes], up),
                copies.start(target.at[:, 32:64, lanes], target.at[:, 160:192, lanes], down),
            ]

    project(0)
    locals_[4].wait()
    for lanes in THIRDS:
        q[:, lanes] = (dot_nn(act[...], weights[2, :, lanes]) * wide(gaps[...])).astype(BF)
    stores.start(q, q_out)
    wait_all(halos[0])
    stores.start(kx, kx_out)
    picks = quad_masks(BF)
    for b in range(2):
        for n in range(3):
            lanes = THIRDS[n]
            total = None
            for s in range(4):
                heads = spread_heads(q[SLAB * s + 64 * b : SLAB * s + 64 * b + 64, lanes], picks)
                term = dot_nt(heads, kx[s, 64 * b : 64 * b + 128, lanes])
                total = term if total is None else total + term
            scores[256 * (3 * b + n) : 256 * (3 * b + n) + 256, :] = total
    got = exchange(spot, copies, lambda i: scores.at[pl.ds(pl.multiple_of(96 * i, 32), 96)], lambda me, k: arrived.at[k])
    project(1)
    rows = masks_in[pl.ds(pl.multiple_of(64 * lax.div(g, 8), 64), 64), :]
    mask_pick[0:64, :] = rows
    mask_pick[64:128, :] = rows
    allowed = mask_pick[pl.ds(pl.multiple_of(32 * lax.rem(g, 2), 32), 96), :]
    wait_all(got)
    mine = pl.ds(pl.multiple_of(96 * g, 32), 96)
    total = scores[mine, :]
    for k in range(1, GROUP):
        total = total + arrived[k]
    total = jnp.where(allowed > 0.5, total * scale, NEG_FILL)
    expo = jnp.exp(total - jnp.max(total, axis=-1, keepdims=True))
    share = expo / jnp.sum(expo, axis=-1, keepdims=True)
    probs[mine, :] = share.astype(BF)
    got = exchange(spot, copies, lambda i: probs.at[mine], lambda me, k: probs.at[mine])
    own[...] = share
    wait_all(halos[1])
    stores.start(vx, vx_out)
    wait_all(got)
    stores.start(probs, probs_out)
    picks = quad_masks(F32)
    at = pl.ds(pl.multiple_of(32 * g, 32), 32)
    got = []
    for dz in (1, 3, 2, 0):
        target = mod4(spot["z"] + dz)
        b, low = lax.div(target, 2), 32 * lax.rem(target, 2)
        for n, lanes in enumerate(THIRDS):
            weigh = jnp.concatenate(
                [probs[pl.ds(pl.multiple_of(256 * (3 * b + n) + 64 * h + low, 32), 32), :] for h in range(4)], axis=0
            )
            for pair in range(2):
                made = [
                    gather_heads(
                        dot_nn(weigh, vx[2 * pair + t, pl.ds(pl.multiple_of(64 * b, 64), 128), lanes]), picks
                    )
                    for t in range(2)
                ]
                for j in range(4):
                    outgoing[4 * target + j, 16 * pair : 16 * pair + 16, lanes] = jnp.concatenate(
                        [m[8 * j : 8 * j + 8] for m in made], axis=0
                    ).astype(BF)
        for dx in range(4):
            if 4 * dz + dx > 0:
                device, index = slab_peer(spot, 4 * dz + dx)
                got.append(copies.start(outgoing.at[index], mixed.at[at], device))
    stores.start(outgoing.at[g], mixed.at[at])
    wait_all(got)
    copies.finish()
    stores.finish()


def vmem_spec():
    return pl.BlockSpec(memory_space=pltpu.VMEM)


def any_spec():
    return pl.BlockSpec(memory_space=pl.ANY)


def row_forward(x, aux, wq, wk, wv, row_gain, row_shift, scale):
    sds = jax.ShapeDtypeStruct
    n_copies = 15 * 5 + 12
    shapes = [
        ((TOKENS, LANES), BF), ((TOKENS, LANES), BF), ((4, REACH, LANES), BF), ((4, REACH, LANES), BF), ((1536, SLAB), BF),
    ]
    return pl.pallas_call(
        functools.partial(row_forward_kernel, scale),
        out_shape=(
            sds((TOKENS, LANES), BF), *[sds(*shape) for shape in shapes], sds((96, SLAB), F32), sds((TOKENS, SLAB), F32),
        ),
        in_specs=[any_spec()] * 5 + [vmem_spec()] * 2,
        out_specs=(any_spec(),) * 6 + (vmem_spec(), any_spec()),
        scratch_shapes=[
            pltpu.VMEM((GROUP, 32, LANES), BF),
            pltpu.VMEM((GROUP, 48, SLAB), BF),
            pltpu.VMEM((3, LANES, LANES), BF),
            pltpu.VMEM((TOKENS, LANES), BF),
            pltpu.VMEM((SLAB, SLAB), F32),
            pltpu.VMEM((SLAB, SLAB), F32),
            pltpu.VMEM((1536, SLAB), F32),
            pltpu.VMEM((GROUP, 96, SLAB), F32),
            pltpu.VMEM((GROUP, 32, LANES), BF),
            *[pltpu.VMEM(*shape) for shape in shapes],
            pltpu.VMEM((TOKENS, SLAB), F32),
            pltpu.VMEM((8, LANES), F32),
            pltpu.SemaphoreType.DMA((n_copies,)),
            pltpu.SemaphoreType.DMA((n_copies,)),
            pltpu.SemaphoreType.DMA((5,)),
            pltpu.SemaphoreType.DMA((8,)),
        ],
        compiler_params=pltpu.CompilerParams(collective_id=1, has_side_effects=True, vmem_limit_bytes=60 * 2**20),
    )(x, aux, wq, wk, wv, row_gain, row_shift)


def row_backward_kernel(
    scale, dm, xrow_in, q_in, kx_in, vx_in, probs_in, gaps_in, wq_in, wk_in, wv_in, squares, *rest
):
    own, row_gain, row_shift, vectors, up_bias, back, sum_col, sum_row, small_out, *rest = rest
    (
        din, dmr, act_t, partial_p, arrived, grads_s, own_k, own_v, edge_out, edge_in, gq, gk, gv, grad_act, outgoing,
        weights, small, halves, slots, vecs, xrow, q, kx, vx, probs, gaps, row_weights,
        col_total, send_sem, recv_sem, local_sem, store_sem, *groups,
    ) = rest
    spot = place()
    g = slab_place(spot)
    copies = Copies(send_sem, recv_sem)
    stores = Stores(store_sem)
    loads = [
        pltpu.make_async_copy(src, dst, local_sem.at[n])
        for n, (src, dst) in enumerate((
            (xrow_in, xrow), (dm.at[g], din.at[g]), (vx_in, vx), (probs_in, probs), (q_in, q), (kx_in, kx), (gaps_in, gaps),
            (wq_in, row_weights.at[0]), (wk_in, row_weights.at[1]), (wv_in, row_weights.at[2]),
        ))
    ]
    for copy in loads:
        copy.start()
    vector_rows(vecs, (row_gain, row_shift))
    gain, shift = vecs.at[0:1], vecs.at[1:2]
    greet(spot, slab_reach(spot)[:15] + [shifted(spot, "y", k) for k in (1, 2, 3)] + [shifted(spot, "aln", 1)])
    got = exchange(spot, copies, lambda i: dm.at[i], lambda me, k: din.at[me])

    first = start_group(spot, copies, groups[:5], squares, col_total, None, sum_col, COL_ORDERS)
    loads[0].wait()

    def normed(k, carry):
        at = pl.ds(pl.multiple_of(128 * k, 128), 128)
        scaled, _ = centre(xrow[at, :].astype(F32))
        act_t[:, at] = jnp.transpose(scaled * gain[...] + shift[...]).astype(BF)
        return carry

    lax.fori_loop(0, 4, normed, 0)
    step_all(*first)
    loads[1].wait()
    wait_all(got)

    def regroup(k, carry):
        first = din[2 * k].astype(F32)
        second = din[2 * k + 1].astype(F32)
        for s in range(4):
            at = pl.ds(pl.multiple_of(SLAB * s + 16 * k, 16), 16)
            dmr[at, :] = jnp.concatenate([first[8 * s : 8 * s + 8], second[8 * s : 8 * s + 8]], axis=0).astype(BF)
        return carry

    lax.fori_loop(0, 8, regroup, 0)
    low_picks = quad_masks(BF)
    picks = quad_masks(F32)
    mine = pl.ds(pl.multiple_of(96 * g, 32), 96)
    loads[2].wait()

    def rows_of(s, b):
        return slice(SLAB * s + 64 * b, SLAB * s + 64 * b + 64)

    for b in range(2):
        for n in range(3):
            lanes = slice(256 * n, 256 * n + 256)
            total = None
            for s in range(4):
                term = dot_nt(spread_heads(dmr[rows_of(s, b), lanes], low_picks), vx[s, 64 * b : 64 * b + 128, lanes])
                total = term if total is None else total + term
            partial_p[256 * (3 * b + n) : 256 * (3 * b + n) + 256, :] = total.astype(BF)
    got = exchange(spot, copies, lambda i: partial_p.at[pl.ds(pl.multiple_of(96 * i, 32), 96)], lambda me, k: arrived.at[k])
    step_all(*first)
    loads[3].wait()
    up, down = shifted(spot, "y", 1), shifted(spot, "y", -1)

    def scatter(weigh, source, target, which, factor):
        edges = []
        for n in range(3):
            lanes = slice(256 * n, 256 * n + 256)
            turned = [
                jnp.transpose(weigh[256 * (3 * b + n) : 256 * (3 * b + n) + 256, :].astype(F32)).astype(BF) for b in range(2)
            ]
            for s in range(4):
                first, second = [
                    dot_nn(turned[b], spread_heads(source[rows_of(s, b), lanes], low_picks)) * factor for b in range(2)
                ]
                edge_out[which, 0, s, :, lanes] = first[0:32].astype(BF)
                target[s, 0:32, lanes] = first[32:64]
                target[s, 32:96, lanes] = first[64:128] + second[0:64]
                target[s, 96:128, lanes] = second[64:96]
                edge_out[which, 1, s, :, lanes] = second[96:128].astype(BF)
            edges += [
                copies.start(edge_out.at[which, 0, :, :, lanes], edge_in.at[which, 0, :, :, lanes], down),
                copies.start(edge_out.at[which, 1, :, :, lanes], edge_in.at[which, 1, :, :, lanes], up),
            ]
        return edges

    edges_v = scatter(probs, dmr, own_v, 0, 1.0)
    step_all(*first)
    wait_all(got)
    total = partial_p[mine, :].astype(F32)
    for k in range(1, GROUP):
        total = total + arrived[k].astype(F32)
    share = own[...]
    grads_s[mine, :] = (share * (total - jnp.sum(share * total, axis=-1, keepdims=True))).astype(BF)
    got = exchange(spot, copies, lambda i: grads_s.at[mine], lambda me, k: grads_s.at[mine])

    def collect(edges, which, source, target):
        wait_all(edges)
        for s in range(4):
            own_rows = source[s]
            first = own_rows[0:32] + edge_in[which, 1, s].astype(F32)
            last = own_rows[96:128] + edge_in[which, 0, s].astype(F32)
            joined = jnp.concatenate([first, own_rows[32:96], last], axis=0)
            if which == 1:
                weigh = gaps[SLAB * s : SLAB * s + SLAB, :]
                joined = joined * jnp.concatenate([weigh] * 6, axis=1)
            target[SLAB * s : SLAB * s + SLAB, :] = joined.astype(BF)

    def weight_grad(n, grad):
        for lanes in THIRDS:
            for at in THIRDS:
                weights[n, at, lanes] = dot_nn(act_t[at, :], grad[:, lanes]).astype(BF)

    collect(edges_v, 0, own_v, gv)
    weight_grad(2, gv)
    for copy in loads[4:7]:
        copy.wait()
    step_all(*first)
    wait_all(got)
    edges_k = scatter(grads_s, q, own_k, 1, scale)
    step_all(*first)
    for b in range(2):
        for n, lanes in enumerate(THIRDS):
            weigh = grads_s[256 * (3 * b + n) : 256 * (3 * b + n) + 256, :]
            for s in range(4):
                made = gather_heads(dot_nn(weigh, kx[s, 64 * b : 64 * b + 128, lanes]), picks) * scale
                gq[rows_of(s, b), lanes] = (made * wide(gaps[rows_of(s, b), :])).astype(BF)
    weight_grad(0, gq)
    collect(edges_k, 1, own_k, gk)
    weight_grad(1, gk)
    last = start_group(spot, copies, groups[5:], weights, weights, spot["aln"] * HALF, sum_row, ROW_ORDERS)
    step_all(*first)
    for copy in loads[7:10]:
        copy.wait()
    wq, wk, wv = [row_weights.at[n] for n in range(3)]
    for at in THIRDS:
        grad_act[:, at] = (
            dot_nt(gq[...], wq[at, :]) + dot_nt(gk[...], wk[at, :]) + dot_nt(gv[...], wv[at, :])
        )
    step_all(*last)

    def norm_back(k, carry):
        grad_gain, grad_shift = carry
        made = []
        for s in range(4):
            at = pl.ds(pl.multiple_of(SLAB * s + 16 * k, 16), 16)
            scaled, inverse = centre(xrow[at, :].astype(F32))
            upstream = grad_act[at, :]
            product = upstream * scaled
            grad_gain = grad_gain + product[0:8] + product[8:16]
            grad_shift = grad_shift + upstream[0:8] + upstream[8:16]
            inner = upstream * gain[...]
            middle = inner - jnp.mean(inner, axis=-1, keepdims=True)
            middle = middle - scaled * jnp.mean(inner * scaled, axis=-1, keepdims=True)
            made.append(inverse * middle)
        for pair in range(2):
            for t in range(2):
                outgoing[2 * k + t, 16 * pair : 16 * pair + 16, :] = jnp.concatenate(
                    [m[8 * t : 8 * t + 8] for m in made[2 * pair : 2 * pair + 2]], axis=0
                ).astype(BF)
        return grad_gain, grad_shift

    zero = jnp.zeros((8, LANES), F32)
    grad_gain, grad_shift = lax.fori_loop(0, 8, norm_back, (zero, zero))
    at = pl.ds(pl.multiple_of(32 * g, 32), 32)
    got = exchange(spot, copies, lambda i: outgoing.at[i], lambda me, k: back.at[at])
    stores.start(outgoing.at[g], back.at[at])
    bias_rows = [
        jnp.concatenate([up_bias[:, HALF * j : HALF * j + HALF], up_bias[:, HALF * (j + 4) : HALF * (j + 5)]], axis=1)
        for j in range(4)
    ]
    sums_here = [jnp.sum(v, axis=0, keepdims=True) for v in (grad_gain, grad_shift)]
    small[...] = jnp.concatenate(
        sums_here + [vectors[0:5, :]] + bias_rows + [jnp.zeros((5, LANES), F32)], axis=0
    )
    finish_all(*last, *first, Run(sum_small(spot, copies, small, halves, slots)))
    wait_all(got)
    copies.finish()
    stores.finish()
    small_out[...] = halves[3]


COL_ORDERS = (("y", "z", "x"), ("y", "x", "z"), ("z", "y", "x"))
ROW_ORDERS = (("x", "y", "z"), ("y", "z", "x"), ("z", "x", "y"))


def rows_of_half(which):
    return pl.ds(pl.multiple_of(which * HALF, HALF), HALF)


def row_backward(dm, kept, wq, wk, wv, squares, own, row_gain, row_shift, vectors, up_bias, scale):
    sds = jax.ShapeDtypeStruct
    n_copies = 15 * 4 + 12 + 2 * GROUP_COPIES + SMALL_COPIES
    low = pltpu.VMEM((TOKENS, LANES), BF)
    reach = pltpu.VMEM((4, REACH, LANES), BF)
    return pl.pallas_call(
        functools.partial(row_backward_kernel, scale),
        out_shape=(
            sds((TOKENS, LANES), BF), sds((5, HALF, LANES), BF), sds((3, HALF, LANES), BF), sds((16, HALF), F32),
        ),
        in_specs=[any_spec()] * 11 + [vmem_spec()] * 5,
        out_specs=(any_spec(),) * 3 + (vmem_spec(),),
        scratch_shapes=[
            pltpu.VMEM((GROUP, 32, LANES), BF),
            low,
            pltpu.VMEM((LANES, TOKENS), BF),
            pltpu.VMEM((1536, SLAB), BF),
            pltpu.VMEM((GROUP, 96, SLAB), BF),
            pltpu.VMEM((1536, SLAB), BF),
            pltpu.VMEM((4, SLAB, LANES), F32),
            pltpu.VMEM((4, SLAB, LANES), F32),
            pltpu.VMEM((2, 2, 4, 32, LANES), BF),
            pltpu.VMEM((2, 2, 4, 32, LANES), BF),
            low,
            low,
            low,
            pltpu.VMEM((TOKENS, LANES), F32),
            pltpu.VMEM((GROUP, 32, LANES), BF),
            pltpu.VMEM((3, LANES, LANES), BF),
            pltpu.VMEM((16, LANES), F32),
            pltpu.VMEM((4, 16, HALF), F32),
            pltpu.VMEM((13, 16, HALF), F32),
            pltpu.VMEM((8, LANES), F32),
            low,
            low,
            reach,
            reach,
            pltpu.VMEM((1536, SLAB), BF),
            pltpu.VMEM((TOKENS, SLAB), F32),
            pltpu.VMEM((3, LANES, LANES), BF),
            pltpu.VMEM((5, HALF, LANES), BF),
            pltpu.SemaphoreType.DMA((n_copies,)),
            pltpu.SemaphoreType.DMA((n_copies,)),
            pltpu.SemaphoreType.DMA((10,)),
            pltpu.SemaphoreType.DMA((1,)),
            *group_scratch(5),
            *group_scratch(3),
        ],
        compiler_params=pltpu.CompilerParams(collective_id=2, has_side_effects=True, vmem_limit_bytes=60 * 2**20),
    )(dm, *kept, wq, wk, wv, squares, own, row_gain, row_shift, vectors, up_bias)


TOKENS = 512
TILE = 256
THIRDS = [slice(256 * n, 256 * n + 256) for n in range(3)]


def to_columns():
    row = lax.broadcasted_iota(jnp.int32, (TOKENS, TOKENS), 0)
    token = lax.broadcasted_iota(jnp.int32, (TOKENS, TOKENS), 1)
    want = lax.rem(row, 64) * 8 + lax.div(row, 64)
    return (token == want).astype(F32).astype(BF)


def to_sequences():
    row = lax.broadcasted_iota(jnp.int32, (TOKENS, TOKENS), 0)
    token = lax.broadcasted_iota(jnp.int32, (TOKENS, TOKENS), 1)
    want = lax.rem(row, 8) * 64 + lax.div(row, 8)
    return (token == want).astype(F32).astype(BF)


def rows_loop(count, body, init=0):
    def step(k, carry):
        return body(pl.ds(pl.multiple_of(64 * k, 64), 64), carry)

    return lax.fori_loop(0, count // 64, step, init)


def normed_rows(values, gain, shift, act, act_t):
    def body(k, carry):
        at = pl.ds(pl.multiple_of(128 * k, 128), 128)
        scaled, _ = centre(values[at, :])
        made = scaled * gain[...] + shift[...]
        act[at, :] = made.astype(BF)
        if act_t is not None:
            act_t[:, at] = jnp.transpose(made).astype(BF)
        return carry

    lax.fori_loop(0, TOKENS // 128, body, 0)


def norm_back_rows(values, upstream, gain, residual, out):
    def body(at, carry):
        grad_gain, grad_shift = carry
        scaled, inverse = centre(values[at, :])
        up = upstream[at, :]
        product = up * scaled
        for r in range(8):
            grad_gain = grad_gain + product[8 * r : 8 * r + 8]
            grad_shift = grad_shift + up[8 * r : 8 * r + 8]
        inner = up * gain[...]
        middle = inner - jnp.mean(inner, axis=-1, keepdims=True)
        middle = middle - scaled * jnp.mean(inner * scaled, axis=-1, keepdims=True)
        out[at, :] = residual[at, :].astype(F32) + inverse * middle
        return grad_gain, grad_shift

    zero = jnp.zeros((8, LANES), F32)
    return rows_loop(TOKENS, body, (zero, zero))


def column_probs(scale, queries, keys, at, lanes, picks):
    heads = spread_heads(queries[at, lanes], picks)
    scores = dot_nt(keys[at, lanes], heads) * scale
    expo = jnp.exp(scores - jnp.max(scores, axis=0, keepdims=True))
    return heads, expo / jnp.sum(expo, axis=0, keepdims=True)


def column_kernel(
    scale, x, mixed, cot, wq, wk, wv, col_out, row_out, up, down,
    col_gain, col_shift, mlp_gain, mlp_shift, down_bias_in, up_bias_in,
    result_out, grad_inputs_out, grad_row_mixed_out, squares_out, sum_mlp, vectors, grad_up_bias,
    squares, vecs, up_bias, weights, up_tiles, down_tiles, raw, order, mixed_cs, act, act_t, after_row, after_col, made, grad_act,
    queries, keys, values, col_mixed, cot_cs, keep, give, load_sem, tile_sem, out_sem, send_sem, recv_sem, *groups,
):
    spot = place()
    side = spot["aln"]
    copies = Copies(send_sem, recv_sem)
    stores = Stores(out_sem)
    vector_rows(vecs, (col_gain, col_shift, mlp_gain, mlp_shift, down_bias_in))
    up_bias[...] = up_bias_in[...].reshape(1, 4 * LANES)
    loads = [
        pltpu.make_async_copy(src, dst, load_sem.at[n])
        for n, (src, dst) in enumerate((
            (mixed, raw.at[1]), (x, raw.at[0]), (row_out, weights.at[4]), (wq, weights.at[0]), (wk, weights.at[1]),
            (wv, weights.at[2]), (col_out, weights.at[3]), (cot, raw.at[2]),
        ))
    ]
    for copy in loads:
        copy.start()
    steps = 2 * 2 * 3

    def spot_of(j):
        half = side if (j // 3) % 2 == 0 else 1 - side
        return half, pl.multiple_of(half * (4 * HALF) + (j // 6) * LANES + (j % 3) * TILE, TILE)

    def fetch(j):
        _, at = spot_of(j)
        slot = j % 3
        return [
            pltpu.make_async_copy(up.at[:, pl.ds(at, TILE)], up_tiles.at[slot], tile_sem.at[slot, 0]),
            pltpu.make_async_copy(down.at[pl.ds(at, TILE)], down_tiles.at[slot], tile_sem.at[slot, 1]),
        ]

    greet(spot, torus_reach(spot))
    order[...] = to_columns()
    loads[0].wait()
    for lanes in THIRDS:
        mixed_cs[:, lanes] = dot_nn(order[...], raw[1, :, lanes]).astype(BF)
    loads[1].wait()
    loads[2].wait()
    for lanes in THIRDS:
        after_row[:, lanes] = dot_nn(order[...], raw[0, :, lanes]) + dot_nn(mixed_cs[...], weights[4, :, lanes])
    normed_rows(after_row, vecs.at[0:1], vecs.at[1:2], act, None)
    for j in range(2):
        for copy in fetch(j):
            copy.start()
    for n, out in enumerate((queries, keys, values)):
        loads[3 + n].wait()
        for lanes in THIRDS:
            out[:, lanes] = dot_nn(act[...], weights[n, :, lanes]).astype(BF)
    low_picks, picks = quad_masks(BF), quad_masks(F32)

    def attend(k, carry):
        for at, lanes in [
            (pl.ds(pl.multiple_of(256 * k + 64 * c, 64), 64), lanes) for c in range(4) for lanes in THIRDS
        ]:
            _, probs = column_probs(scale, queries, keys, at, lanes, low_picks)
            mixes = dot_tn(probs.astype(BF), values[at, lanes])
            col_mixed[at, lanes] = gather_heads(mixes, picks).astype(BF)
        return carry

    lax.fori_loop(0, 2, attend, 0)
    loads[6].wait()
    for lanes in THIRDS:
        after_col[:, lanes] = after_row[:, lanes] + dot_nn(col_mixed[...], weights[3, :, lanes])
    gain, shift, down_bias = vecs.at[2:3], vecs.at[3:4], vecs.at[4:5]
    normed_rows(after_col, gain, shift, act, act_t)
    loads[7].wait()
    for lanes in THIRDS:
        cot_cs[:, lanes] = dot_nn(order[...], raw[2, :, lanes]).astype(BF)
    order[...] = to_sequences()

    def mlp_group(i):
        return start_group(
            spot, copies, groups[5 * i : 5 * i + 5], (keep.at[i], give.at[i]), keep.at[i], 0, sum_mlp.at[i], MLP_ORDERS[i])

    for j in range(steps):
        half, at = spot_of(j)
        slot, i = j % 3, j // 6
        if j + 2 < steps:
            for copy in fetch(j + 2):
                copy.start()
        for copy in fetch(j):
            copy.wait()
        hidden_pre = dot_nn(act[...], up_tiles[slot]) + up_bias[:, pl.ds(at, TILE)]
        grad_hidden = dot_nt(cot_cs[...], down_tiles[slot])
        phi = 0.5 + 0.5 * lax.erf(hidden_pre * (1.0 / math.sqrt(2.0)))
        slope = phi + hidden_pre * jnp.exp(-0.5 * hidden_pre * hidden_pre) * (1.0 / math.sqrt(2.0 * math.pi))
        hidden = (hidden_pre * phi).astype(BF)
        pre = (grad_hidden * slope).astype(BF)
        tall = keep if (j // 3) % 2 == 0 else give
        hidden_t = jnp.transpose(hidden)
        lanes_here = slice(TILE * (j % 3), TILE * (j % 3) + TILE)
        for lanes in THIRDS:
            if j == 0:
                made[:, lanes] = dot_nn(hidden, down_tiles[slot, :, lanes])
                grad_act[:, lanes] = dot_nt(pre, up_tiles[slot, lanes, :])
            else:
                made[:, lanes] += dot_nn(hidden, down_tiles[slot, :, lanes])
                grad_act[:, lanes] += dot_nt(pre, up_tiles[slot, lanes, :])
            grad = dot_nn(hidden_t, cot_cs[:, lanes]).astype(BF)
            for part in range(2):
                low, high = max(TILE * (j % 3), HALF * part), min(TILE * (j % 3) + TILE, HALF * part + HALF)
                if low < high:
                    tall[i, part, low - HALF * part : high - HALF * part, lanes] = (
                        grad[low - TILE * (j % 3) : high - TILE * (j % 3)]
                    )
        for which, out in ((side, keep), (1 - side, give)):
            out[i, 2 + half, :, lanes_here] = dot_nn(act_t[rows_of_half(which), :], pre).astype(BF)
        grad_up_bias[:, pl.ds(at, TILE)] = jnp.sum(pre.astype(F32), axis=0, keepdims=True)
        if j in (7, 10):
            step_all(*first)
        if j == 5:
            first = mlp_group(0)
        if j == 11:
            second = mlp_group(1)
    for lanes in THIRDS:
        full = after_col[:, lanes] + (made[:, lanes] + down_bias[:, lanes])
        raw[2, :, lanes] = dot_nn(order[...], full.astype(BF)).astype(BF)
    stores.start(raw.at[2], result_out)
    sum_gain, sum_shift = norm_back_rows(after_col, grad_act, gain, cot_cs, after_col)

    def bias_sum(at, carry):
        values_here = cot_cs[at, :].astype(F32)
        for r in range(8):
            carry = carry + values_here[8 * r : 8 * r + 8]
        return carry

    bias = rows_loop(TOKENS, bias_sum, jnp.zeros((8, LANES), F32))
    branch, grad_mixed = raw.at[0], raw.at[1]

    def rounded(at, carry):
        branch[at, :] = after_col[at, :].astype(BF)
        return carry

    rows_loop(TOKENS, rounded)
    step_all(*first, *second)
    for lanes in THIRDS:
        grad_mixed[:, lanes] = dot_nt(branch[...], weights[3, lanes, :]).astype(BF)
    gain, shift = vecs.at[0:1], vecs.at[1:2]
    normed_rows(after_row, gain, shift, act, act_t)

    def attend_back(k, carry):
        for at, lanes in [
            (pl.ds(pl.multiple_of(128 * k + 64 * c, 64), 64), lanes) for c in range(2) for lanes in THIRDS
        ]:
            heads, probs = column_probs(scale, queries, keys, at, lanes, low_picks)
            upstream = spread_heads(grad_mixed[at, lanes], low_picks)
            grad_probs = dot_nt(values[at, lanes], upstream)
            grad_scores = probs * (grad_probs - jnp.sum(probs * grad_probs, axis=0, keepdims=True))
            grad_scores = grad_scores.astype(BF)
            gq = (gather_heads(dot_tn(grad_scores, keys[at, lanes]), picks) * scale).astype(BF)
            gk = (dot_nn(grad_scores, heads) * scale).astype(BF)
            gv = dot_nn(probs.astype(BF), upstream).astype(BF)
            queries[at, lanes] = gq
            keys[at, lanes] = gk
            values[at, lanes] = gv
        return carry

    for n, runs in enumerate((first, second, first, second)):
        lax.fori_loop(n, n + 1, attend_back, 0)
        step_all(*runs)
    for lanes in THIRDS:
        grad_act[:, lanes] = (
            dot_nt(queries[...], weights[0, lanes, :])
            + dot_nt(keys[...], weights[1, lanes, :])
            + dot_nt(values[...], weights[2, lanes, :])
        )
    for at in THIRDS:
        squares[0, at, :] = dot_tn(col_mixed[:, at], branch[...]).astype(BF)
    stores.start(squares.at[0], squares_out.at[0])
    step_all(*first, *second)
    grad_gain, grad_shift = norm_back_rows(after_row, grad_act, gain, after_col, after_row)
    sums = [jnp.sum(v, axis=0, keepdims=True) for v in (grad_gain, grad_shift, sum_gain, sum_shift, bias)]
    vectors[...] = jnp.concatenate(sums + [jnp.zeros((3, LANES), F32)], axis=0)

    def rounded_row(at, carry):
        values_here = after_row[at, :]
        high = values_here.astype(BF)
        branch[at, :] = high
        act[at, :] = (values_here - high.astype(F32)).astype(BF)
        return carry

    rows_loop(TOKENS, rounded_row)
    for lanes in THIRDS:
        grad_mixed[:, lanes] = dot_nt(branch[...], weights[4, lanes, :]).astype(BF)
    for lanes in THIRDS:
        cot_cs[:, lanes] = dot_nn(order[...], grad_mixed[:, lanes]).astype(BF)
        made[:, lanes] = dot_nn(order[...], branch[:, lanes]) + dot_nn(order[...], act[:, lanes])
    stores.start(cot_cs, grad_row_mixed_out)
    stores.start(made, grad_inputs_out)
    step_all(*first, *second)
    for n, grad in enumerate((queries, keys, values)):
        for at in THIRDS:
            squares[1 + n, at, :] = dot_nn(act_t[at, :], grad[...]).astype(BF)
        stores.start(squares.at[1 + n], squares_out.at[1 + n])
    step_all(*second)
    for at in THIRDS:
        squares[4, at, :] = dot_tn(mixed_cs[:, at], branch[...]).astype(BF)
    stores.start(squares.at[4], squares_out.at[4])
    finish_all(*first, *second)
    copies.finish()
    stores.finish()


MLP_ORDERS = (
    (("x", "y", "z"), ("y", "z", "x"), ("z", "x", "y")),
    (("x", "z", "y"), ("y", "x", "z"), ("z", "y", "x")),
)


def column_part(
    x, mixed, cot, wq, wk, wv, col_out, row_out, up, down, col_gain, col_shift, mlp_gain, mlp_shift, down_bias, up_bias, scale
):
    sds = jax.ShapeDtypeStruct
    hidden = up.shape[1]
    tokens = sds((TOKENS, LANES), BF)
    low = pltpu.VMEM((TOKENS, LANES), BF)
    full = pltpu.VMEM((TOKENS, LANES), F32)
    n_copies = 2 * GROUP_COPIES
    return pl.pallas_call(
        functools.partial(column_kernel, scale),
        out_shape=(
            tokens, sds((TOKENS, LANES), F32), tokens, sds((5, LANES, LANES), BF), sds((2, 4, HALF, LANES), BF),
            sds((8, LANES), F32), sds((1, hidden), F32),
        ),
        in_specs=[any_spec()] * 10 + [vmem_spec()] * 6,
        out_specs=(any_spec(),) * 5 + (vmem_spec(),) * 2,
        scratch_shapes=[
            pltpu.VMEM((5, LANES, LANES), BF),
            pltpu.VMEM((8, LANES), F32),
            pltpu.VMEM((1, hidden), F32),
            pltpu.VMEM((5, LANES, LANES), BF),
            pltpu.VMEM((3, LANES, TILE), BF),
            pltpu.VMEM((3, TILE, LANES), BF),
            pltpu.VMEM((3, TOKENS, LANES), BF),
            pltpu.VMEM((TOKENS, TOKENS), BF),
            low, low, pltpu.VMEM((LANES, TOKENS), BF), full, full, full, full, low, low, low, low, low,
            pltpu.VMEM((2, 4, HALF, LANES), BF),
            pltpu.VMEM((2, 4, HALF, LANES), BF),
            pltpu.SemaphoreType.DMA((8,)),
            pltpu.SemaphoreType.DMA((3, 2)),
            pltpu.SemaphoreType.DMA((8,)),
            pltpu.SemaphoreType.DMA((n_copies,)),
            pltpu.SemaphoreType.DMA((n_copies,)),
            *group_scratch(4),
            *group_scratch(4),
        ],
        compiler_params=pltpu.CompilerParams(collective_id=3, has_side_effects=True, vmem_limit_bytes=60 * 2**20),
    )(
        x, mixed, cot, wq, wk, wv, col_out, row_out, up, down,
        col_gain, col_shift, mlp_gain, mlp_shift, down_bias, up_bias,
    )


def finish_kernel(base, back, mlp, col, row, small, total, up, down, *rest):
    squares, vectors, bias = rest[:8], rest[8:15], rest[15]
    total[...] = base[...] + back[...].astype(F32)
    for i in range(2):
        for n in range(2):
            down[2 * i + n] = mlp[i, n].astype(F32)
            k = 2 * n + i
            up[:, LANES * k : LANES * k + LANES] = mlp[i, 2 + n].astype(F32)
    for n in range(5):
        squares[n][...] = col[n].astype(F32)
    for n in range(3):
        squares[5 + n][...] = row[n].astype(F32)
    for n in range(7):
        vectors[n][...] = small[n, :]
    for n in range(4):
        bias[HALF * n : HALF * n + HALF] = small[7 + n, :]


def finish(base, back, mlp, col, row, small):
    steps = 8
    rows = HALF // steps
    sds = jax.ShapeDtypeStruct
    tokens = pl.BlockSpec((TOKENS // steps, LANES), lambda i: (i, 0))
    square = pl.BlockSpec((rows, LANES), lambda i: (i, 0))
    return pl.pallas_call(
        finish_kernel,
        grid=(steps,),
        out_shape=[
            sds((TOKENS, LANES), F32), sds((HALF, 4 * LANES), F32), sds((4, HALF, LANES), F32),
            *[sds((HALF, LANES), F32)] * 8, *[sds((HALF,), F32)] * 7, sds((4 * HALF,), F32),
        ],
        in_specs=[
            tokens, tokens,
            pl.BlockSpec((2, 4, rows, LANES), lambda i: (0, 0, i, 0)),
            pl.BlockSpec((5, rows, LANES), lambda i: (0, i, 0)),
            pl.BlockSpec((3, rows, LANES), lambda i: (0, i, 0)),
            pl.BlockSpec((16, HALF), lambda i: (0, 0)),
        ],
        out_specs=[
            tokens,
            pl.BlockSpec((rows, 4 * LANES), lambda i: (i, 0)),
            pl.BlockSpec((4, rows, LANES), lambda i: (0, i, 0)),
            *[square] * 8, *[pl.BlockSpec((HALF,), lambda i: (0,))] * 7, pl.BlockSpec((4 * HALF,), lambda i: (0,)),
        ],
        compiler_params=pltpu.CompilerParams(vmem_limit_bytes=60 * 2**20),
    )(base, back, mlp, col, row, small)


def side_inputs(gap_flags, band_mask):
    col = lax.axis_index("col")
    weights = (1.0 - GAP_DROP * gap_flags.astype(F32)).reshape(GROUP, 32, 1)
    query = 8 * lax.rem(col, 8) + jnp.arange(8, dtype=jnp.int32)[:, None]
    key = jnp.arange(SLAB, dtype=jnp.int32)[None, :]
    offset = key - query
    chosen = (offset[:, :, None] == jnp.arange(2 * BAND + 1, dtype=jnp.int32)) & (band_mask[:, None, :] == 1)
    where = 64 * lax.div(col, 8) + key - BAND
    allowed = (jnp.any(chosen, axis=-1) | (offset == BAND)) & (where >= 0) & (where < COLS)
    allowed = jnp.broadcast_to(allowed.astype(F32)[None], (GROUP, 8, SLAB))
    weights = jnp.broadcast_to(weights, (GROUP, 32, SLAB))
    return jnp.concatenate([weights, allowed, jnp.zeros((GROUP, 8, SLAB), F32)], axis=1).astype(BF)


def per_device(
    inputs,
    gap_flags,
    band_mask,
    row_gain,
    row_shift,
    row_query,
    row_key,
    row_value,
    row_out,
    col_gain,
    col_shift,
    col_query,
    col_key,
    col_value,
    col_out,
    mlp_gain,
    mlp_shift,
    mlp_up,
    up_bias,
    mlp_down,
    down_bias,
    cotangent,
):
    seqs, width_cols, model = (inputs.shape[1], inputs.shape[2], inputs.shape[3])
    low_tokens = (seqs * width_cols, model)
    row_scale = 1.0 / math.sqrt(HD * seqs)
    col_scale = 1.0 / math.sqrt(HD)
    aux = side_inputs(gap_flags[0], band_mask[0])
    mixed_low, *kept_row, own, gaps = row_forward(
        inputs.reshape(GROUP, 32, model), aux, row_query, row_key, row_value, row_gain, row_shift, row_scale
    )
    result, grad_after_row, grad_row_mixed, squares, sum_mlp, vectors, grad_up_bias = column_part(
        inputs.reshape(low_tokens), mixed_low, cotangent.reshape(low_tokens), col_query, col_key, col_value, col_out,
        row_out, mlp_up, mlp_down, col_gain, col_shift, mlp_gain, mlp_shift, down_bias, up_bias, col_scale,
    )
    back_row, sum_col, sum_row, small_sum = row_backward(
        grad_row_mixed.reshape(GROUP, 32, model), (*kept_row, gaps), row_query, row_key, row_value, squares, own, row_gain,
        row_shift, vectors, grad_up_bias, row_scale,
    )
    grad_inputs, up_sum, down_sum, co_sum, cq_sum, ck_sum, cv_sum, ro_sum, rq_sum, rk_sum, rv_sum, *vector_sums = finish(
        grad_after_row, back_row, sum_mlp, sum_col, sum_row, small_sum
    )
    return (
        result.reshape(inputs.shape),
        grad_inputs.reshape(inputs.shape),
        vector_sums[0],
        vector_sums[1],
        rq_sum,
        rk_sum,
        rv_sum,
        ro_sum,
        vector_sums[2],
        vector_sums[3],
        cq_sum,
        ck_sum,
        cv_sum,
        co_sum,
        vector_sums[4],
        vector_sums[5],
        up_sum,
        vector_sums[7],
        down_sum.reshape(4 * HALF, model),
        vector_sums[6],
    )


def solution(mesh):
    in_specs = (
        P("aln", None, "col", None),
        P("aln", None, "col"),
        P("aln", "col", None),
        P(),
        P(),
        P(),
        P(),
        P(),
        P(),
        P(),
        P(),
        P(),
        P(),
        P(),
        P(),
        P(),
        P(),
        P(),
        P(),
        P(),
        P(),
        P("aln", None, "col", None),
    )
    out_specs = (
        P("aln", None, "col", None),
        P("aln", None, "col", None),
        P("aln"),
        P("aln"),
        P("aln", None),
        P("aln", None),
        P("aln", None),
        P("aln", None),
        P("aln"),
        P("aln"),
        P("aln", None),
        P("aln", None),
        P("aln", None),
        P("aln", None),
        P("aln"),
        P("aln"),
        P("aln", None),
        P("aln"),
        P("aln", None),
        P("aln"),
    )
    return jax.shard_map(
        per_device, mesh=mesh, in_specs=in_specs, out_specs=out_specs, check_vma=False
    )
```
